32 devices in a mesh: face: 4 (over y, core), tile: 8 (over z, x).
Axes of the slice: x: 2, y: 2, z: 4, core: 2. Of those that a mesh axis runs over, the one named last changes fastest.
Arguments:
- met_src: bfloat16 [2048, 48, 128], P(('face', 'tile')), may hold values from -6 to 6
- intersection_weights: bfloat16 [2048, 128, 128], P(('face', 'tile')), may hold values from -0.5 to 0.5
- block_dest: int32 [2048], P(('face', 'tile')), may hold values from 0 to 31, as said below
- block_row: int32 [2048], P(('face', 'tile')), may hold values from 0 to 15
- tracers: float32 [250, 4, 64, 1024], P(None, None, 'face', 'tile'), may hold values from 0.1 to 10
- rate_coef: float32 [250, 12], replicated, may hold values from -1.75 to 1.75
- photo_coef: float32 [250], replicated, may hold values from 0.1 to 3
Outputs:
- met_tile: float32 [12, 4, 64, 1024], P(None, None, 'face', 'tile')
- species_out: float32 [250, 4, 64, 1024], P(None, None, 'face', 'tile')
The draws below stay inside these ranges and needn't reach their ends.
Inputs may be any that keep to these rules, and one draw needn't show every extreme that they name: `block_dest`: each source owner (the 64 blocks of one device) names any one tile owner at most 2 times; in every draw some tile owner is named exactly 2 times by every source owner.
All inputs are finite; a program needn't handle non-finite values.
Results may differ from the reference program's by a relative error of at most 0.0029.
Values may be sent and summed in bfloat16 or wider, within the bound.
No kernel may reach another device: no remote copies, remote signals or barrier semaphores. Data moves between devices by JAX's collectives and lax.ppermute only.
A program may use at most 128 MiB of HBM per device.

```python
import math
import jax
import jax.numpy as jnp
from jax import lax

NFLD = 12
NSPEC = 250
LEV = 4
TY = 128
TX = 16
CAP = 2
ADV_STEPS = 2
SB = 64
SRCBLK = 2048
FL = 48
NX = 64
NY = 1024
N_FACE = 4
N_TILE = 8


def draw_block_dest(key, part):
    owners = N_FACE * N_TILE
    hottest = jax.random.randint(jax.random.fold_in(key, 7), (), 0, owners)

    def one_source(source_key):
        others = jax.random.permutation(source_key, owners - 1)
        shuffle = jax.random.permutation(jax.random.fold_in(source_key, 3), SB)
        position = jnp.arange(SB)
        group_index = jnp.clip((position - CAP) // CAP, 0, owners - 2)
        chosen = jnp.where(position < CAP, hottest, (hottest + 1 + others[group_index]) % owners)
        return chosen[shuffle]
    source_keys = jax.random.split(jax.random.fold_in(key, 11), owners)
    return jax.vmap(one_source)(source_keys).reshape(owners * SB).astype(jnp.int32)


def set_ends(entries, rng, low, high):
    index_at = [jax.random.randint(jax.random.fold_in(rng, axis), (), 0, length) for axis, length in enumerate(entries.shape)]
    longest = entries.shape.index(max(entries.shape))
    beside = index_at[:longest] + [(index_at[longest] + 1) % entries.shape[longest]] + index_at[longest + 1:]
    return entries.at[tuple(index_at)].set(low).at[tuple(beside)].set(high)


def steps_of(key, extent, cuts, low, top_value):
    def one(dim, parts):
        steps = jax.random.uniform(jax.random.fold_in(jax.random.fold_in(key, 6), dim), (parts,), jnp.float32, low / len(cuts), top_value / len(cuts))
        return jnp.repeat(jnp.exp(steps), extent[dim] // parts).reshape((-1,) + (1,) * (len(extent) - dim - 1))

    factor_of = one(*cuts[0])
    for cut in cuts[1:]:
        factor_of = factor_of * one(*cut)
    return factor_of


def normal_values(rng, shape, width, limit, pieces=(), dtype=jnp.bfloat16):
    result = width * jax.random.normal(rng, shape, jnp.float32)
    if pieces:
        result = result * steps_of(rng, shape, pieces, -0.22, 0.18)
    return jnp.clip(result, -limit, limit).astype(dtype)


def setup_inputs(seed: int = 0) -> dict:
    splits = jax.random.split(jax.random.key(seed), 8)
    return {
        "met_src": normal_values(splits[0], (SRCBLK, FL, TY), 1.0, 6.0, ((0, 32),)),
        "intersection_weights": normal_values(splits[1], (SRCBLK, TY, TY), TY ** -0.5, 0.5, ((0, 32),)),
        "block_dest": draw_block_dest(jax.random.fold_in(splits[7], 71), 0),
        "block_row": set_ends(jax.random.randint(splits[3], (SRCBLK,), 0, TX), jax.random.fold_in(splits[3], 1), 0, TX - 1).astype(jnp.int32),
        "tracers": jnp.clip(jnp.exp(math.log(10.0) - 4.6051702 * jax.random.uniform(splits[4], (NSPEC, LEV, NX, NY), jnp.float32) ** steps_of(splits[4], (NSPEC, LEV, NX, NY), ((2, 4), (3, 8)), -0.2, 0.2)), 0.1, 10.0),
        "rate_coef": normal_values(splits[5], (NSPEC, NFLD), NFLD ** -0.5, 1.75, (), jnp.float32),
        "photo_coef": jnp.clip(jnp.exp(jax.random.uniform(splits[6], (NSPEC,), jnp.float32, math.log(0.1), math.log(3.0))), 0.1, 3.0),
    }


def reference(met_src, intersection_weights, block_dest, block_row, tracers, rate_coef, photo_coef):
    products = jnp.einsum("sfi,sij->sfj", met_src.astype(jnp.float32), intersection_weights.astype(jnp.float32), precision=lax.Precision.HIGHEST)
    products = lax.optimization_barrier(products.astype(jnp.bfloat16)).astype(jnp.float32)
    target_rows = (block_dest * TX + block_row).astype(jnp.int32)
    summed = jax.ops.segment_sum(products, target_rows, num_segments=N_FACE * N_TILE * TX)
    met_tile = summed.reshape(N_FACE, N_TILE, TX, NFLD, LEV, TY).transpose(3, 4, 0, 2, 1, 5).reshape(NFLD, LEV, NX, NY)
    courant_x = 0.3 * jnp.tanh(met_tile[0])
    courant_y = 0.3 * jnp.tanh(met_tile[1])
    column_depth = jnp.cumsum(jax.nn.softplus(met_tile[2]), axis=0)
    light = jnp.exp(-column_depth)

    def one_species(species_item):
        amount, coefficients, photolysis = species_item
        for substep in range(ADV_STEPS):
            flux_x = jnp.maximum(courant_x, 0.0) * amount + jnp.minimum(courant_x, 0.0) * jnp.roll(amount, -1, axis=1)
            flux_y = jnp.maximum(courant_y, 0.0) * amount + jnp.minimum(courant_y, 0.0) * jnp.roll(amount, -1, axis=2)
            amount = amount - (flux_x - jnp.roll(flux_x, 1, axis=1)) - (flux_y - jnp.roll(flux_y, 1, axis=2))
        exponent = jnp.einsum("f,flxy->lxy", coefficients, met_tile, precision=lax.Precision.HIGHEST) + photolysis * light
        return amount / (1.0 + jax.nn.softplus(exponent))

    species_out = lax.map(one_species, (tracers, rate_coef, photo_coef))
    return met_tile, species_out
```

```python
import functools

import jax
import jax.numpy as jnp
from jax import lax
from jax.experimental import pallas as pl
from jax.experimental.pallas import tpu as pltpu
from jax.sharding import PartitionSpec as P

CAP = 2
F32 = jnp.float32
BF16 = jnp.bfloat16
HALF = 128
ROW_GROUP = 4
BIG = 50
BIGGEST = 60
MIB = 1024 * 1024
SMEM = pltpu.MemorySpace.SMEM


def here(count):
    return [pl.BlockSpec(memory_space=pl.ANY)] * count


def params(mib):
    return pltpu.CompilerParams(vmem_limit_bytes=mib * MIB)


def buffers(arrays):
    return [pltpu.VMEM(x.shape, x.dtype) for x in arrays]


def fetch(sources, targets, sems):
    copies = [pltpu.make_async_copy(s, t, sems.at[i]) for i, (s, t) in enumerate(zip(sources, targets))]
    for copy in copies:
        copy.start()
    return copies


def finish(copies):
    for copy in copies:
        copy.wait()


def lanes(shape):
    return lax.broadcasted_iota(jnp.int32, shape, len(shape) - 1)


def sublanes(shape):
    return lax.broadcasted_iota(jnp.int32, shape, len(shape) - 2)


def turn(x, shift):
    count = x.shape[-1]
    shift = shift % count
    return x if shift == 0 else pltpu.roll(x, shift, x.ndim - 1)


def regrid_kernel(rows, dest_any, row_any, src_any, weight_any, tracer_any,
                  first_any, second_any, top_any, bottom_any,
                  dest_ref, row_ref, src_ref, weight_ref, first_ref, second_ref, border, top_ref, bottom_ref,
                  index_ref, count_ref, sems, border_sems):
    owners = first_ref.shape[0]
    levels = top_ref.shape[1]
    species = tracer_any.shape[0]
    blocks, levfields, cells = src_ref.shape
    copies = fetch([dest_any, row_any, src_any, weight_any], [dest_ref, row_ref, src_ref, weight_ref], sems)
    wanted = [(level, row) for level in range(levels) for row in (0, 1, rows - 2, rows - 1)]
    lines = fetch(
        [tracer_any.at[:, level * rows + row, 0, :] for level, row in wanted],
        [border.at[i, pl.ds(0, species), :] for i in range(len(wanted))], border_sems,
    )

    def clear(d, carry):
        count_ref[d] = 0
        for k in range(CAP):
            index_ref[d * CAP + k] = -1
        return carry

    lax.fori_loop(0, owners, clear, 0, unroll=8)
    finish(copies[:2])

    def place(b, carry):
        d = dest_ref[b]
        k = count_ref[d]
        index_ref[d * CAP + jnp.minimum(k, CAP - 1)] = b
        count_ref[d] = k + 1
        return carry

    lax.fori_loop(0, blocks, place, 0, unroll=8)
    finish(copies[2:])
    row_id = sublanes((16, cells))
    low_half = sublanes((8, cells)) < 4

    def send(d, carry):
        parts, heads = [], []
        for k in range(CAP):
            b = index_ref[d * CAP + k]
            used = b >= 0
            at = jnp.maximum(b, 0)
            product = jnp.dot(src_ref[at], weight_ref[at], preferred_element_type=F32)
            product = jnp.where(used, product, 0.0)
            label = jnp.where(used, row_ref[at], -1).astype(F32)
            parts.append(product)
            heads.append(jnp.where(row_id < 12, product[0:16], label))
        first_ref[d] = jnp.concatenate(heads, axis=0).astype(BF16)
        mixed = jnp.where(low_half, pltpu.roll(parts[0][8:16], 4, 0), parts[1][8:16])
        second_ref[d] = jnp.concatenate([parts[0][16:], parts[1][16:], mixed], axis=0).astype(BF16)
        return carry

    lax.fori_loop(0, owners, send, 0, unroll=8)
    copies = fetch([first_ref, second_ref], [first_any, second_any], sems)
    finish(lines)
    for i, (level, row) in enumerate(wanted):
        if row < 2:
            top_ref[row, level] = border[i].astype(BF16)
        else:
            bottom_ref[row - rows + 2, level] = border[i].astype(BF16)
    finish(copies + fetch([top_ref, bottom_ref], [top_any, bottom_any], border_sems))


def regrid(block_dest, block_row, met_src, weights, planes, owners, padded, levels, rows):
    blocks, levfields, cells = met_src.shape
    line = jax.ShapeDtypeStruct((2, levels, padded, cells), BF16)
    first = jax.ShapeDtypeStruct((owners, CAP * 16, cells), BF16)
    second = jax.ShapeDtypeStruct((owners, CAP * (levfields - 12), cells), BF16)
    return pl.pallas_call(
        functools.partial(regrid_kernel, rows),
        out_shape=(first, second, line, line),
        in_specs=here(5),
        out_specs=tuple(here(4)),
        scratch_shapes=[
            pltpu.SMEM(block_dest.shape, jnp.int32), pltpu.SMEM(block_row.shape, jnp.int32),
            *buffers([met_src, weights, first, second]),
            pltpu.VMEM((4 * levels, padded, cells), F32), *buffers([line, line]),
            pltpu.SMEM((owners * CAP,), jnp.int32), pltpu.SMEM((owners,), jnp.int32),
            pltpu.SemaphoreType.DMA((4,)), pltpu.SemaphoreType.DMA((4 * levels,)),
        ],
        compiler_params=params(BIGGEST),
        cost_estimate=pl.CostEstimate(
            flops=2 * blocks * levfields * cells * cells, bytes_accessed=6 * MIB, transcendentals=0
        ),
        name="regrid",
    )(block_dest, block_row, met_src, weights, planes)


def load_planes(source, target, sems):
    species = source.shape[0]
    copies = []
    for k in range(source.shape[1]):
        copy = pltpu.make_async_copy(source.at[:, k, 0, :], target.at[k, pl.ds(0, species), :], sems.at[k])
        copy.start()
        copies.append(copy)
    return copies


def column_kernel(levels, tracer_any, right_ref, left_ref, planes, total, picker, sems):
    count, padded, cells = planes.shape
    rows = count // levels
    load_planes(tracer_any, planes, sems)
    total[...] = jnp.zeros_like(total)
    picker[...] = jnp.zeros_like(picker)
    sub, lane = sublanes((16, 2 * cells)), lanes((16, 2 * cells))

    def one_level(level, carry):
        for row in range(rows):
            pltpu.make_async_copy(
                tracer_any.at[:, level * rows + row, 0, :],
                planes.at[level * rows + row, pl.ds(0, tracer_any.shape[0]), :],
                sems.at[level * rows + row],
            ).wait()
        for row in range(0, rows, 2):
            pair = []
            for h in range(2):
                k = level * rows + row + h
                pair.append(planes[k].astype(BF16))
                low = (sub < 2) & (lane == cells + 2 * k + sub)
                high = (sub >= 14) & (lane == 2 * k + sub - 14)
                picker[row // 2, pl.ds(h * cells, 16), :] = jnp.where(low, 1.0, 0.0).astype(BF16)
                picker[row // 2, pl.ds((h + 1) * cells - 16, 16), :] = jnp.where(high, 1.0, 0.0).astype(BF16)
            both = jnp.concatenate(pair, axis=1)
            total[...] += jnp.dot(both, picker[row // 2], preferred_element_type=F32)
        return carry

    lax.fori_loop(0, levels, one_level, 0)
    right_ref[...] = total[:, 0:cells].astype(BF16)
    left_ref[...] = total[:, cells:].astype(BF16)


def columns(planes, padded, levels):
    _, count, _, cells = planes.shape
    side = jax.ShapeDtypeStruct((padded, cells), BF16)
    return pl.pallas_call(
        functools.partial(column_kernel, levels),
        out_shape=(side, side),
        in_specs=here(1),
        scratch_shapes=[
            pltpu.VMEM((count, padded, cells), F32),
            pltpu.VMEM((padded, 2 * cells), F32), pltpu.VMEM((count // levels // 2, 2 * cells, 2 * cells), BF16),
            pltpu.SemaphoreType.DMA((count,)),
        ],
        compiler_params=params(BIG),
        cost_estimate=pl.CostEstimate(flops=12 * planes.size, bytes_accessed=4 * planes.size, transcendentals=0),
        name="columns",
    )(planes)


def softplus(x):
    return jnp.maximum(x, 0.0) + jnp.log(1.0 + jnp.exp(-jnp.abs(x)))


def first_fields_kernel(levels, first_any, met_any, courant_any, last_any, zero_any, light_any, label_ref,
                        first_ref, met_ref, courant_ref, light_ref, label_v, label_s, sems):
    owners, _, cells = first_ref.shape
    rows = met_ref.shape[0]
    finish(fetch([first_any], [first_ref], sems))

    def gather(d, carry):
        x = first_ref[d].astype(F32)
        found = [x[16 * k + 12 : 16 * k + 13] for k in range(CAP)]
        label_v[pl.ds(d * CAP, CAP), :] = jnp.concatenate(found, axis=0).astype(jnp.int32)
        return carry

    lax.fori_loop(0, owners, gather, 0, unroll=8)
    labels = fetch([label_v], [label_s], sems)
    keep = sublanes((16, cells)) < 12

    def add(d, sums):
        x = first_ref[d].astype(F32)
        sums = list(sums)
        for k in range(CAP):
            part = jnp.where(keep, x[16 * k : 16 * k + 16], 0.0)
            label = jnp.broadcast_to(x[16 * k + 12 : 16 * k + 13], (16, cells))
            for r in range(rows):
                sums[r] += jnp.where(label == r, part, 0.0)
        return tuple(sums)

    zero = jnp.zeros((16, cells), F32)
    sums = lax.fori_loop(0, owners, add, (zero,) * rows)
    for r in range(rows):
        met_ref[r] = sums[r]
        courant_ref[r] = 0.3 * jnp.tanh(sums[r][0 : 2 * levels])
    copies = fetch(
        [courant_ref, courant_ref.at[pl.ds(rows - 2, 2)], courant_ref.at[pl.ds(0, 1)], met_ref],
        [courant_any, last_any, zero_any, met_any], sems.at[pl.ds(1, 4)],
    )
    depth = softplus(met_ref[:, 2 * levels : 4 * levels, :])
    parts = []
    running = jnp.zeros((rows, 1, cells), F32)
    for level in range(levels):
        running = running + depth[:, level : level + 1]
        parts.append(jnp.exp(-running))
    parts.append(jnp.zeros((rows, 8 - levels, cells), F32))
    light_ref[...] = jnp.concatenate(parts, axis=1)
    finish(labels)
    copies += fetch([light_ref], [light_any], sems)

    def keep_label(i, carry):
        label = label_s[i, 0]
        label_ref[i] = jnp.where(label < 0, rows, label)
        return carry

    lax.fori_loop(0, owners * CAP, keep_label, 0, unroll=8)
    finish(copies)


def first_fields(first, levels, rows):
    owners, _, cells = first.shape
    outs = (
        jax.ShapeDtypeStruct((rows, 16, cells), F32),
        jax.ShapeDtypeStruct((rows, 2 * levels, cells), F32),
        jax.ShapeDtypeStruct((rows, 8, cells), F32),
    )
    last = jax.ShapeDtypeStruct((2, 2 * levels, cells), F32)
    zero = jax.ShapeDtypeStruct((1, 2 * levels, cells), F32)
    return pl.pallas_call(
        functools.partial(first_fields_kernel, levels),
        out_shape=(outs[0], outs[1], last, zero, outs[2], jax.ShapeDtypeStruct((owners * CAP,), jnp.int32)),
        in_specs=here(1),
        out_specs=(*here(5), pl.BlockSpec(memory_space=SMEM)),
        scratch_shapes=[
            *buffers([first, *outs]),
            pltpu.VMEM((owners * CAP, cells), jnp.int32),
            pltpu.SMEM((owners * CAP, cells), jnp.int32),
            pltpu.SemaphoreType.DMA((5,)),
        ],
        compiler_params=params(6),
        cost_estimate=pl.CostEstimate(flops=MIB, bytes_accessed=2 * MIB, transcendentals=MIB // 8),
        name="first_fields",
    )(first)


def ghost_lines(courant_ref, below_ref, above_ref):
    rows = courant_ref.shape[0]
    return [below_ref[0], below_ref[1]] + [courant_ref[r] for r in range(rows)] + [above_ref[0]]


def edge_kernel(below_any, above_any, right_any, left_any, courant_any, cbelow_any, cabove_any,
                right_out, left_out, cright_out,
                below_ref, above_ref, right_two, left_two, courant_ref, cbelow_ref, cabove_ref, cright_ref, sems):
    levels, padded, cells = below_ref.shape
    fields = cright_ref.shape[0]
    span = cells // levels
    copies = fetch(
        [courant_any, cbelow_any, cabove_any, below_any.at[1], above_any.at[0], right_any, left_any],
        [courant_ref, cbelow_ref, cabove_ref, below_ref, above_ref,
         right_two.at[pl.ds(0, padded)], left_two.at[pl.ds(0, padded)]], sems,
    )
    finish(copies[:3])
    pair = lanes((fields, cells)) // 2
    right = jnp.zeros((fields, cells), F32)
    left = jnp.zeros((fields, cells), F32)
    for k, x in enumerate(ghost_lines(courant_ref, cbelow_ref, cabove_ref)):
        moved = turn(x, 2 * k - (cells - 2))
        right = jnp.where(pair == k, moved, right)
        left = jnp.where(pair == k + 1, moved, left)
    left = turn(left, -2)
    cright_ref[...] = right
    for ref, x in ((right_two, right), (left_two, left)):
        high = x.astype(BF16).astype(F32)
        ref[pl.ds(2 * padded, 2 * fields), :] = jnp.concatenate([high, x - high], axis=0).astype(BF16)
    finish(copies[3:])
    pair = lanes((padded, cells)) // 2
    corner_right = jnp.zeros((padded, cells), F32)
    corner_left = jnp.zeros((padded, cells), F32)
    for level in range(levels):
        for ref, k in ((below_ref, level * span // 2), (above_ref, (level + 1) * span // 2 - 1)):
            moved = turn(ref[level].astype(F32), 2 * k - (cells - 2))
            corner_right = jnp.where(pair == k, moved, corner_right)
            corner_left = jnp.where(pair == (k + 1) % (cells // 2), moved, corner_left)
    right_two[pl.ds(padded, padded), :] = corner_right.astype(BF16)
    left_two[pl.ds(padded, padded), :] = turn(corner_left, -2).astype(BF16)
    finish(fetch([right_two, left_two, cright_ref], [right_out, left_out, cright_out], sems))


def edges(below, above, right, left, courant, cbelow, cabove):
    levels, padded, cells = below.shape[1:]
    fields = courant.shape[1]
    side = jax.ShapeDtypeStruct((2 * padded + 2 * fields, cells), BF16)
    line = jax.ShapeDtypeStruct((levels, padded, cells), BF16)
    own = jax.ShapeDtypeStruct((fields, cells), F32)
    return pl.pallas_call(
        edge_kernel,
        out_shape=(side, side, own),
        in_specs=here(7),
        out_specs=tuple(here(3)),
        scratch_shapes=[
            *buffers([line, line, side, side, courant, cbelow, cabove, own]), pltpu.SemaphoreType.DMA((7,))
        ],
        compiler_params=params(8),
        cost_estimate=pl.CostEstimate(flops=below.size, bytes_accessed=2 * MIB, transcendentals=0),
        name="edges",
    )(below, above, right, left, courant, cbelow, cabove)


def five_weights(face_x, face_x_low, face_y, face_y_low):
    up = -jnp.minimum(face_x, 0.0)
    down = jnp.maximum(face_x_low, 0.0)
    right = -jnp.minimum(face_y, 0.0)
    left = jnp.maximum(face_y_low, 0.0)
    stay = (
        1.0
        - (jnp.maximum(face_x, 0.0) - jnp.minimum(face_x_low, 0.0))
        - (jnp.maximum(face_y, 0.0) - jnp.minimum(face_y_low, 0.0))
    )
    return stay, up, down, left, right


def spread(x, level, count):
    return jnp.broadcast_to(x[level : level + 1], (count, x.shape[1]))


def make_weights(levels, courant_ref, below_ref, above_ref, own_right, west, east, inner, side, edge):
    rows, fields, cells = courant_ref.shape
    lane = lanes((fields, cells))
    line = ghost_lines(courant_ref, below_ref, above_ref)
    for i in range(1, rows + 3):
        now, low = line[i], line[i - 1]
        face_y_low = jnp.where(lane == 0, turn(west, -(2 * i + 1)), turn(now, 1))[levels:]
        five = five_weights(now[:levels], low[:levels], now[levels:], face_y_low)
        for level in range(levels):
            for c in range(3):
                inner[level, i - 1, c] = spread(five[c], level, 8)
            for c in range(2):
                side[level, i - 1, c] = spread(five[3 + c], level, 16).astype(BF16)
    odd = lane % 2 == 1
    middle = jnp.where(odd, west, east)
    lower = turn(middle, 2)
    y_low = jnp.where(odd, turn(west, 1), turn(own_right, -1))
    stay, up, down, left, right = five_weights(
        middle[:levels], lower[:levels], middle[levels:], y_low[levels:]
    )
    odd = odd[:levels]
    outer_w = jnp.where(odd, left, right)
    inner_w = jnp.where(odd, right, left)
    lane8 = lanes((8, cells))
    span = cells // levels
    for c, x in enumerate((stay, up, down, outer_w, inner_w)):
        out = jnp.zeros((8, cells), F32)
        for level in range(levels):
            out = jnp.where(lane8 // span == level, turn(spread(x, level, 8), level * span - 4), out)
        edge[c] = out


def side_columns(rows, levels, right_ref, left_ref, west_ref, east_ref, edge, mid_ref, corner_ref, next_ref):
    padded, cells = right_ref.shape
    span = cells // levels
    lane = lanes((16, cells))
    odd = lane % 2 == 1
    row_of = (lane % span) // 2

    def group(g, carry):
        part = pl.ds(pl.multiple_of(g * 16, 16), 16)
        corner_part = pl.ds(pl.multiple_of(padded + g * 16, 16), 16)
        lo, lo_c = west_ref[part, :].astype(F32), west_ref[corner_part, :].astype(F32)
        hi, hi_c = east_ref[part, :].astype(F32), east_ref[corner_part, :].astype(F32)
        own_r, own_l = right_ref[part, :].astype(F32), left_ref[part, :].astype(F32)
        weights = [jnp.concatenate([edge[c]] * 2, axis=0) for c in range(5)]
        mid = jnp.where(odd, lo, hi)
        corner = jnp.where(odd, lo_c, hi_c)
        outside = jnp.where(odd, turn(lo, 1), turn(hi, -1))
        inside = jnp.where(odd, turn(own_l, 1), turn(own_r, -1))
        above = jnp.where(row_of == rows - 1, corner, turn(mid, -2))
        below = jnp.where(row_of == 0, corner, turn(mid, 2))
        mid_ref[part, :] = mid.astype(BF16)
        corner_ref[part, :] = corner.astype(BF16)
        after = (
            weights[0] * mid + weights[1] * above + weights[2] * below
            + weights[3] * outside + weights[4] * inside
        )
        next_ref[part, :] = after.astype(BF16)
        return carry

    lax.fori_loop(0, padded // 16, group, 0)


def advect_kernel(
    levels, tracer_any, below_any, above_any, right_any, left_any, west_any, east_any,
    courant_any, cbelow_any, cabove_any, cright_any, out_any,
    planes, below_ref, above_ref, right_ref, left_ref, west_ref, east_ref,
    courant_ref, cbelow_ref, cabove_ref, cright_ref,
    inner, side, edge, mid_ref, corner_ref, next_ref, matrix, low_mask, high_mask, once, once16,
    plane_sems, in_sems, out_sems,
):
    rows, _, cells = courant_ref.shape
    padded = planes.shape[1]
    span = cells // levels
    small = fetch(
        [courant_any, cbelow_any, cabove_any, cright_any, west_any, east_any,
         right_any, left_any, below_any, above_any],
        [courant_ref, cbelow_ref, cabove_ref, cright_ref, west_ref, east_ref,
         right_ref, left_ref, below_ref, above_ref], in_sems,
    )
    loads = load_planes(tracer_any, planes, plane_sems)
    sub, lane = sublanes((cells, cells)), lanes((cells, cells))
    low_mask[...] = jnp.where(sub == lane - 1, 1.0, 0.0).astype(BF16)
    high_mask[...] = jnp.where(sub == lane + 1, 1.0, 0.0).astype(BF16)
    finish(small[:6])
    fields = cright_ref.shape[0]
    cwest, ceast = (
        ref[pl.ds(2 * padded, fields), :].astype(F32) + ref[pl.ds(2 * padded + fields, fields), :].astype(F32)
        for ref in (west_ref, east_ref)
    )
    make_weights(levels, courant_ref, cbelow_ref, cabove_ref, cright_ref[...], cwest, ceast, inner, side, edge)
    finish(small[6:])
    side_columns(rows, levels, right_ref, left_ref, west_ref, east_ref, edge, mid_ref, corner_ref, next_ref)
    sub16, lane16 = sublanes((16, cells)), lanes((16, cells))

    def set_matrix(level, i):
        left, right = side[level, i + 1, 0], side[level, i + 1, 1]
        for t in range(cells // 16):
            at = pl.ds(16 * t, 16)
            matrix[i + 1, at, :] = low_mask[at, :] * left + high_mask[at, :] * right
        matrix[i + 1, pl.ds(cells, cells), :] = jnp.zeros((cells, cells), BF16)
        p = 2 * min(max(i, 0), rows - 1)
        tile = jnp.where(
            (sub16 == p % 16 + 1) & (lane16 == 0), left.astype(F32),
            jnp.where((sub16 == p % 16) & (lane16 == cells - 1), right.astype(F32), 0.0),
        )
        at = pl.multiple_of(cells + level * span + p // 16 * 16, 16)
        matrix[i + 1, pl.ds(at, 16), :] = tile.astype(BF16)

    def weighted(weights, x, up, down):
        count = x.shape[0] // 8
        stay, up_w, down_w = (w[None] for w in weights)
        x, up, down = (v.reshape(count, 8, cells) for v in (x, up, down))
        return (stay * x + up_w * up + down_w * down).reshape(count * 8, cells)

    def one_level(level, carry):
        for r in range(rows):
            pltpu.make_async_copy(
                tracer_any.at[:, level * rows + r, 0, :],
                planes.at[level * rows + r, pl.ds(0, tracer_any.shape[0]), :],
                plane_sems.at[level * rows + r],
            ).wait()
        for i in range(-1, rows + 1):
            set_matrix(level, i)

        def half(b, carry):
            part = pl.ds(pl.multiple_of(b * HALF, HALF), HALF)

            def before(i):
                if i < 0:
                    return below_ref[i + 2, level, part, :].astype(F32)
                if i >= rows:
                    return above_ref[i - rows, level, part, :].astype(F32)
                return planes[level * rows + i, part, :]

            for i in range(-1, rows + 1):
                x = before(i)
                beside = (mid_ref if 0 <= i < rows else corner_ref)[part, :]
                both = jnp.concatenate([x.astype(BF16), beside], axis=1)
                across = jnp.dot(both, matrix[i + 1], preferred_element_type=F32)
                weights = [inner[level, i + 1, c] for c in range(3)]
                x = weighted(weights, x, before(i + 1), before(i - 1)) + across
                once[i + 1] = x
                if 0 <= i < rows:
                    once16[i] = x.astype(BF16)
            for i in range(rows):
                both = jnp.concatenate([once16[i], next_ref[part, :]], axis=1)
                across = jnp.dot(both, matrix[i + 1], preferred_element_type=F32)
                weights = [inner[level, i + 1, c] for c in range(3)]
                planes[level * rows + i, part, :] = (
                    weighted(weights, once[i + 1], once[i + 2], once[i]) + across
                )
            return carry

        lax.fori_loop(0, padded // HALF, half, 0)
        for r in range(rows):
            pltpu.make_async_copy(
                planes.at[level * rows + r], out_any.at[level * rows + r], out_sems.at[level * rows + r]
            ).start()
        return carry

    lax.fori_loop(0, levels, one_level, 0)
    for k in range(levels * rows):
        pltpu.make_async_copy(planes.at[k], out_any.at[k], out_sems.at[k]).wait()


def advect(planes, below, above, right, left, west, east, courant, cbelow, cabove, cright):
    levels, padded, cells = below.shape[1:]
    rows = courant.shape[0]
    small = [below, above, right, left, west, east, courant, cbelow, cabove, cright]
    count = levels * rows
    column = pltpu.VMEM((padded, cells), BF16)
    square = pltpu.VMEM((cells, cells), BF16)
    return pl.pallas_call(
        functools.partial(advect_kernel, levels),
        out_shape=jax.ShapeDtypeStruct((count, padded, cells), F32),
        in_specs=here(1 + len(small)),
        out_specs=here(1)[0],
        scratch_shapes=[
            pltpu.VMEM((count, padded, cells), F32),
            *buffers(small),
            pltpu.VMEM((levels, rows + 2, 3, 8, cells), F32),
            pltpu.VMEM((levels, rows + 2, 2, 16, cells), BF16),
            pltpu.VMEM((5, 8, cells), F32),
            column, column, column,
            pltpu.VMEM((rows + 2, 2 * cells, cells), BF16),
            square, square,
            pltpu.VMEM((rows + 2, HALF, cells), F32),
            pltpu.VMEM((rows, HALF, cells), BF16),
            pltpu.SemaphoreType.DMA((count,)), pltpu.SemaphoreType.DMA((len(small),)),
            pltpu.SemaphoreType.DMA((count,)),
        ],
        compiler_params=params(BIG),
        cost_estimate=pl.CostEstimate(
            flops=40 * planes.size, bytes_accessed=8 * planes.size, transcendentals=0
        ),
        name="advect",
    )(planes, *small)


def chemistry_kernel(levels, label_any, second_any, met_any, light_any, rate_any, moved_any, out_any, tile_any,
                     label_ref, second_ref, met_ref, light_ref, rate_ref, planes, tile_ref, total, factor,
                     in_sems, plane_sems, out_sems):
    owners, _, cells = second_ref.shape
    count = planes.shape[0]
    rows = count // levels
    species = out_any.shape[0]
    levfields = total.shape[0] // (rows + 1)
    small = fetch(
        [label_any, second_any, met_any, light_any, rate_any],
        [label_ref, second_ref, met_ref, light_ref, rate_ref], in_sems,
    )
    for r in range(rows):
        for level in range(levels):
            k = level * rows + r
            pltpu.make_async_copy(moved_any.at[k], planes.at[k], plane_sems.at[k]).start()
    finish(small)
    for r in range(rows):
        total[pl.ds(r * levfields, 16), :] = met_ref[r]
        total[pl.ds(r * levfields + 16, levfields - 16), :] = jnp.zeros((levfields - 16, cells), F32)
    total[pl.ds(rows * levfields, levfields), :] = jnp.zeros((levfields, cells), F32)
    low_half = sublanes((8, cells)) < 4

    def add(d, carry):
        x = second_ref[d].astype(F32)
        many = levfields - 16
        mixed = x[CAP * many :]
        extra = [jnp.where(low_half, 0.0, pltpu.roll(mixed, 4, 0)), jnp.where(low_half, 0.0, mixed)]
        for k in range(CAP):
            at = pl.multiple_of(label_ref[d * CAP + k] * levfields, 8)
            total[pl.ds(at + 8, 8), :] += extra[k]
            total[pl.ds(at + 16, many), :] += x[k * many : (k + 1) * many]
        return carry

    lax.fori_loop(0, owners, add, 0, unroll=4)
    for r in range(rows):
        x = jnp.concatenate(
            [total[pl.ds(r * levfields, levfields), :], light_ref[r], jnp.zeros((8, cells), F32)], axis=0
        )
        high = x.astype(BF16)
        rest = (x - high.astype(F32)).astype(BF16)
        factor[r] = jnp.concatenate([high, rest, high], axis=0)

    def some_rows(c, carry):
        for dr in range(ROW_GROUP):
            for level in range(levels):
                k = level * rows + c * ROW_GROUP + dr
                pltpu.make_async_copy(moved_any.at[k], planes.at[k], plane_sems.at[k]).wait()
        for dr in range(ROW_GROUP):
            r = c * ROW_GROUP + dr
            for level in range(levels):
                k = level * rows + r
                exponent = jnp.dot(rate_ref[level], factor[r], preferred_element_type=F32)
                planes[k] = planes[k] * pl.reciprocal(1.0 + softplus(exponent), approx=False)
        for dr in range(ROW_GROUP):
            for level in range(levels):
                k = level * rows + c * ROW_GROUP + dr
                pltpu.make_async_copy(
                    planes.at[k, pl.ds(0, species), :], out_any.at[:, k, 0, :], out_sems.at[k]
                ).start()
        return carry

    lax.fori_loop(0, rows // ROW_GROUP, some_rows, 0)
    for fl in range(levfields):
        for r in range(0, rows, 8):
            tile_ref[fl, pl.ds(r, 8), :] = total[pl.ds(r * levfields + fl, 8, stride=levfields), :]
    finish(fetch([tile_ref], [tile_any], in_sems))
    for k in range(count):
        pltpu.make_async_copy(
            planes.at[k, pl.ds(0, species), :], out_any.at[:, k, 0, :], out_sems.at[k]
        ).wait()


def chemistry(labels, second, met, light, rate, moved, levels, species):
    owners, _, cells = second.shape
    count, padded, _ = moved.shape
    rows = count // levels
    levfields = second.shape[1] // CAP + 12
    depth = rate.shape[2]
    tile = jax.ShapeDtypeStruct((levfields, rows, cells), F32)
    return pl.pallas_call(
        functools.partial(chemistry_kernel, levels),
        out_shape=(jax.ShapeDtypeStruct((species, count, 1, cells), F32), tile),
        in_specs=here(6),
        out_specs=tuple(here(2)),
        scratch_shapes=[
            pltpu.SMEM(labels.shape, jnp.int32),
            *buffers([second, met, light, rate, moved, tile]),
            pltpu.VMEM(((rows + 1) * levfields, cells), F32),
            pltpu.VMEM((rows, depth, cells), BF16),
            pltpu.SemaphoreType.DMA((5,)), pltpu.SemaphoreType.DMA((count,)), pltpu.SemaphoreType.DMA((count,)),
        ],
        compiler_params=params(BIG),
        cost_estimate=pl.CostEstimate(
            flops=20 * moved.size, bytes_accessed=8 * moved.size, transcendentals=3 * moved.size
        ),
        name="chemistry",
    )(labels, second, met, light, rate, moved)


def rate_factors(rate_coef, photo_coef, levels, padded):
    species, fields = rate_coef.shape
    same = jnp.eye(levels, dtype=F32)
    by_field = rate_coef[None, :, :, None] * same[:, None, None, :]
    by_light = photo_coef[None, :, None] * same[:, None, :]
    table = jnp.concatenate([by_field.reshape(levels, species, fields * levels), by_light], axis=2)
    table = jnp.pad(table, ((0, 0), (0, padded - species), (0, 64 - table.shape[2])))
    high = lax.reduce_precision(table, 8, 7)
    rest = (table - high).astype(BF16)
    high = high.astype(BF16)
    return jnp.concatenate([high, high, rest], axis=2)


def shift(x, axis, by):
    count = lax.axis_size(axis)
    return lax.ppermute(x, axis, [(i, (i + by) % count) for i in range(count)])


def local(met_src, intersection_weights, block_dest, block_row, tracers, rate_coef, photo_coef):
    owners = lax.axis_size("face") * lax.axis_size("tile")
    species, levels, rows, cells = tracers.shape
    padded = -(-species // HALF) * HALF
    tracer_planes = tracers.reshape(species, levels * rows, 1, cells)

    first, second, top, bottom = regrid(
        block_dest, block_row, met_src, intersection_weights, tracer_planes, owners, padded, levels, rows
    )
    first = lax.all_to_all(first, ("face", "tile"), split_axis=0, concat_axis=0, tiled=True)
    below = shift(bottom, "face", 1)
    above = shift(top, "face", -1)
    right, left = columns(tracer_planes, padded, levels)

    met, courant, clast, czero, light, labels = first_fields(first, levels, rows)
    second, clast, czero, right, below, above = lax.optimization_barrier(
        (second, clast, czero, right, below, above)
    )
    second = lax.all_to_all(second, ("face", "tile"), split_axis=0, concat_axis=0, tiled=True)
    cbelow = shift(clast, "face", 1)
    cabove = shift(czero, "face", -1)
    right_send, left_send, cright = edges(below, above, right, left, courant, cbelow, cabove)
    west = shift(right_send, "tile", 1)
    east = shift(left_send, "tile", -1)
    moved = advect(tracer_planes, below, above, right, left, west, east, courant, cbelow, cabove, cright)
    rate = rate_factors(rate_coef, photo_coef, levels, padded)
    out, met_tile = chemistry(labels, second, met, light, rate, moved, levels, species)
    fields = rate_coef.shape[1]
    return met_tile.reshape(fields, levels, rows, cells), out.reshape(species, levels, rows, cells)


def solution(mesh):
    return jax.shard_map(
        local,
        mesh=mesh,
        in_specs=(
            P(("face", "tile"), None, None),
            P(("face", "tile"), None, None),
            P(("face", "tile")),
            P(("face", "tile")),
            P(None, None, "face", "tile"),
            P(),
            P(),
        ),
        out_specs=(P(None, None, "face", "tile"), P(None, None, "face", "tile")),
        check_vma=False,
    )
```

```python
import functools

import jax
import jax.numpy as jnp
from jax import lax
from jax.experimental import pallas as pl
from jax.experimental.pallas import tpu as pltpu
from jax.sharding import PartitionSpec as P

CAP = 2
F32 = jnp.float32
BF16 = jnp.bfloat16
HALF = 256
COL = 50
BIG = 50
ADV = 50
BIGGEST = 60
MIB = 1024 * 1024
SMEM = pltpu.MemorySpace.SMEM
VMEM = pltpu.MemorySpace.VMEM


def here(count):
    return [pl.BlockSpec(memory_space=pl.ANY)] * count


def params(mib):
    return pltpu.CompilerParams(vmem_limit_bytes=mib * MIB)


def buffers(arrays):
    return [pltpu.VMEM(x.shape, x.dtype) for x in arrays]


def fetch(sources, targets, sems):
    copies = [pltpu.make_async_copy(s, t, sems.at[i]) for i, (s, t) in enumerate(zip(sources, targets))]
    for copy in copies:
        copy.start()
    return copies


def finish(copies):
    for copy in copies:
        copy.wait()


def lanes(shape):
    return lax.broadcasted_iota(jnp.int32, shape, len(shape) - 1)


def sublanes(shape):
    return lax.broadcasted_iota(jnp.int32, shape, len(shape) - 2)


def turn(x, shift):
    count = x.shape[-1]
    shift = shift % count
    return x if shift == 0 else pltpu.roll(x, shift, x.ndim - 1)


def regrid_kernel(n_tile, rows, dest_any, row_any, src_any, weight_any, out_any,
                  dest_ref, row_ref, src_ref, weight_ref, out_ref, line_ref, column_ref, index_ref, count_ref, sems):
    owners = out_ref.shape[0]
    n_face = owners // n_tile
    blocks, levfields, cells = src_ref.shape
    copies = fetch([dest_any, row_any, src_any, weight_any], [dest_ref, row_ref, src_ref, weight_ref], sems)

    def clear(d, carry):
        count_ref[d] = 0
        for k in range(CAP):
            index_ref[d * CAP + k] = -1
        return carry

    lax.fori_loop(0, owners, clear, 0, unroll=8)
    finish(copies[:2])

    def place(b, carry):
        d = dest_ref[b]
        k = count_ref[d]
        index_ref[d * CAP + jnp.minimum(k, CAP - 1)] = b
        count_ref[d] = k + 1
        return carry

    lax.fori_loop(0, blocks, place, 0, unroll=8)
    finish(copies[2:])
    lane = lanes((8, cells))
    pair = lane // 2
    half = cells // 2
    tail = CAP * levfields

    def product(d, carry):
        zero = jnp.zeros((8, cells), F32)
        west, east, line = zero, zero, [zero, zero, zero]
        labels = zero
        for k in range(CAP):
            b = index_ref[d * CAP + k]
            used = b >= 0
            at = jnp.maximum(b, 0)
            x = jnp.dot(src_ref[at], weight_ref[at], preferred_element_type=F32)
            x = jnp.where(used, x, 0.0).astype(BF16)
            out_ref[d, pl.ds(k * levfields, levfields), :] = x
            head = x[0:16].astype(F32)[0:8]
            row = jnp.where(used, row_ref[at], rows)
            moved = pltpu.roll(head, jnp.mod(2 * row + 6, cells), 1)
            west += jnp.where(pair == row + 2, moved, 0.0)
            east += jnp.where(pair == row + 3, moved, 0.0)
            for n, r in enumerate((rows - 1, 0, rows - 2)):
                line[n] += jnp.where(row == r, head, 0.0)
            labels = jnp.where(lane == 2 * rows + 8 + k, row.astype(F32), labels)
        column = jnp.where(lane < half, west, 0.0) + turn(east, half - 2)
        column_ref[d, 0] = column
        column_ref[d, 1] = turn(column, -2 * rows)
        column_ref[d, 2] = turn(column, 2 * rows)
        column_ref[d, 3] = labels
        for n in range(3):
            line_ref[d, n] = line[n]
        return carry

    lax.fori_loop(0, owners, product, 0, unroll=8)
    inside = lane % half
    in_rows = (inside >= 4) & (inside < 4 + 2 * rows)
    before = (inside >= 2) & (inside < 4)
    after = (inside >= 4 + 2 * rows) & (inside < 6 + 2 * rows)
    is_west = lane < half

    def surround(d, carry):
        f, t = d // n_tile, d % n_tile
        up, down = jnp.where(f == 0, n_face - 1, f - 1), jnp.where(f == n_face - 1, 0, f + 1)
        low, high = jnp.where(t == 0, n_tile - 1, t - 1), jnp.where(t == n_tile - 1, 0, t + 1)
        tile = column_ref[d, 3]
        for side, x in ((is_west, low), (~is_west, high)):
            tile += jnp.where(side & in_rows, column_ref[f * n_tile + x, 0], 0.0)
            tile += jnp.where(side & before, column_ref[up * n_tile + x, 1], 0.0)
            tile += jnp.where(side & after, column_ref[down * n_tile + x, 2], 0.0)
        parts = [tile, line_ref[up * n_tile + t, 0], line_ref[down * n_tile + t, 1], line_ref[up * n_tile + t, 2]]
        out_ref[d, pl.ds(tail, 32), :] = jnp.concatenate(parts, axis=0).astype(BF16)
        return carry

    lax.fori_loop(0, owners, surround, 0, unroll=4)
    finish(fetch([out_ref], [out_any], sems))


def regrid(block_dest, block_row, met_src, weights, n_face, n_tile, rows):
    blocks, levfields, cells = met_src.shape
    owners = n_face * n_tile
    out = jax.ShapeDtypeStruct((owners, CAP * levfields + 32, cells), BF16)
    return pl.pallas_call(
        functools.partial(regrid_kernel, n_tile, rows),
        out_shape=out,
        in_specs=here(4),
        out_specs=here(1)[0],
        scratch_shapes=[
            pltpu.SMEM(block_dest.shape, jnp.int32), pltpu.SMEM(block_row.shape, jnp.int32),
            *buffers([met_src, weights, out]),
            pltpu.VMEM((owners, 3, 8, cells), F32), pltpu.VMEM((owners, 4, 8, cells), F32),
            pltpu.SMEM((owners * CAP,), jnp.int32), pltpu.SMEM((owners,), jnp.int32),
            pltpu.SemaphoreType.DMA((4,)),
        ],
        compiler_params=params(BIGGEST),
        cost_estimate=pl.CostEstimate(
            flops=2 * blocks * levfields * cells * cells, bytes_accessed=6 * MIB, transcendentals=0
        ),
        name="regrid",
    )(block_dest, block_row, met_src, weights)


def own_lanes(padded, cells, width):
    shape = (padded, cells)
    return lanes(shape) // width == sublanes(shape) % 8


def row_kernel(rows, tracer_any, top_any, bottom_any, corner_any, border, top_ref, bottom_ref, corner_ref, sems):
    levels, padded, cells = top_ref.shape[1:]
    species = tracer_any.shape[0]
    width = 4 * levels
    sub, lane = sublanes((cells, cells)), lanes((cells, cells)) % width
    column = jnp.where(lane % 2 == 0, cells - 1, 0)
    spread_out = jnp.zeros((padded, cells), F32)
    wanted = [(level, row) for level in range(levels) for row in (0, 1, rows - 2, rows - 1)]
    finish(fetch(
        [tracer_any.at[:, level * rows + row, 0, :] for level, row in wanted],
        [border.at[i, pl.ds(0, species), :] for i in range(len(wanted))], sems,
    ))
    for i, (level, row) in enumerate(wanted):
        x = border[i].astype(BF16)
        if row < 2:
            top_ref[row, level] = x
        else:
            bottom_ref[row - rows + 2, level] = x
        if row in (0, rows - 1):
            from_row = lane // 2 == 2 * level + (1 if row == 0 else 0)
            select = jnp.where((sub == column) & from_row, 1.0, 0.0).astype(BF16)
            spread_out += jnp.dot(x, select, preferred_element_type=F32)
    packed = jnp.where(own_lanes(padded, cells, width), spread_out, 0.0)
    corner_ref[...] = jnp.sum(packed.reshape(padded // 8, 8, cells), axis=1).astype(BF16)
    finish(fetch([top_ref, bottom_ref, corner_ref], [top_any, bottom_any, corner_any], sems))


def border_rows(planes, padded, levels, rows):
    cells = planes.shape[3]
    line = jax.ShapeDtypeStruct((2, levels, padded, cells), BF16)
    corner = jax.ShapeDtypeStruct((padded // 8, cells), BF16)
    return pl.pallas_call(
        functools.partial(row_kernel, rows),
        out_shape=(line, line, corner),
        in_specs=here(1),
        out_specs=tuple(here(3)),
        scratch_shapes=[
            pltpu.VMEM((4 * levels, padded, cells), F32), *buffers([line, line, corner]),
            pltpu.SemaphoreType.DMA((4 * levels,)),
        ],
        compiler_params=params(BIG),
        cost_estimate=pl.CostEstimate(flops=planes.size, bytes_accessed=planes.size, transcendentals=0),
        name="border_rows",
    )(planes)


def load_planes(source, target, sems):
    species = source.shape[0]
    copies = []
    for k in range(source.shape[1]):
        copy = pltpu.make_async_copy(source.at[:, k, 0, :], target.at[k, pl.ds(0, species), :], sems.at[k])
        copy.start()
        copies.append(copy)
    return copies


def column_kernel(levels, tracer_any, planes_any, right_ref, left_ref, planes, total, picker, sems, out_sems):
    count, padded, cells = planes.shape
    rows = count // levels
    load_planes(tracer_any, planes, sems)
    total[...] = jnp.zeros_like(total)
    picker[...] = jnp.zeros_like(picker)
    sub, lane = sublanes((16, 2 * cells)), lanes((16, 2 * cells))

    def one_level(level, carry):
        for row in range(rows):
            pltpu.make_async_copy(
                tracer_any.at[:, level * rows + row, 0, :],
                planes.at[level * rows + row, pl.ds(0, tracer_any.shape[0]), :],
                sems.at[level * rows + row],
            ).wait()
        part = pl.ds(level * rows, rows)
        pltpu.make_async_copy(planes.at[part], planes_any.at[part], out_sems.at[level]).start()
        for row in range(0, rows, 2):
            pair = []
            for h in range(2):
                k = level * rows + row + h
                pair.append(planes[k].astype(BF16))
                low = (sub < 2) & (lane == cells + 2 * k + sub)
                high = (sub >= 14) & (lane == 2 * k + sub - 14)
                picker[row // 2, pl.ds(h * cells, 16), :] = jnp.where(low, 1.0, 0.0).astype(BF16)
                picker[row // 2, pl.ds((h + 1) * cells - 16, 16), :] = jnp.where(high, 1.0, 0.0).astype(BF16)
            both = jnp.concatenate(pair, axis=1)
            total[...] += jnp.dot(both, picker[row // 2], preferred_element_type=F32)
        return carry

    lax.fori_loop(0, levels, one_level, 0)
    for level in range(levels):
        part = pl.ds(level * rows, rows)
        pltpu.make_async_copy(planes.at[part], planes_any.at[part], out_sems.at[level]).wait()
    right_ref[...] = total[:, 0:cells].astype(BF16)
    left_ref[...] = total[:, cells:].astype(BF16)


def columns(planes, padded, levels):
    _, count, _, cells = planes.shape
    side = jax.ShapeDtypeStruct((padded, cells), BF16)
    return pl.pallas_call(
        functools.partial(column_kernel, levels),
        out_shape=(
            jax.ShapeDtypeStruct((count, padded, cells), F32), side, side,
        ),
        in_specs=here(1),
        out_specs=(*here(1), *[pl.BlockSpec(memory_space=VMEM)] * 2),
        scratch_shapes=[
            pltpu.VMEM((count, padded, cells), F32),
            pltpu.VMEM((padded, 2 * cells), F32), pltpu.VMEM((count // levels // 2, 2 * cells, 2 * cells), BF16),
            pltpu.SemaphoreType.DMA((count,)), pltpu.SemaphoreType.DMA((levels,)),
        ],
        compiler_params=params(COL),
        cost_estimate=pl.CostEstimate(flops=12 * planes.size, bytes_accessed=4 * planes.size, transcendentals=0),
        name="columns",
    )(planes)


def softplus(x):
    return jnp.maximum(x, jnp.log(1.0 + jnp.exp(jnp.minimum(x, 60.0))))


def five_weights(face_x, face_x_low, face_y, face_y_low):
    up = -jnp.minimum(face_x, 0.0)
    down = jnp.maximum(face_x_low, 0.0)
    right = -jnp.minimum(face_y, 0.0)
    left = jnp.maximum(face_y_low, 0.0)
    stay = (
        1.0
        - (jnp.maximum(face_x, 0.0) - jnp.minimum(face_x_low, 0.0))
        - (jnp.maximum(face_y, 0.0) - jnp.minimum(face_y_low, 0.0))
    )
    return stay, up, down, left, right


def spread(x, level, count):
    return jnp.broadcast_to(x[level : level + 1], (count, x.shape[1]))


def make_weights(levels, line, west, east, inner, side, edge):
    rows = len(line) - 3
    fields, cells = line[0].shape
    lane = lanes((fields, cells))
    own_right = jnp.zeros((fields, cells), F32)
    for i in range(2, rows + 2):
        own_right = jnp.where(lane // 2 == i, turn(line[i], 2 * i - (cells - 2)), own_right)
    for i in range(1, rows + 3):
        now, low = line[i], line[i - 1]
        face_y_low = jnp.where(lane == 0, turn(west, -(2 * i + 1)), turn(now, 1))[levels:]
        five = five_weights(now[:levels], low[:levels], now[levels:], face_y_low)
        for level in range(levels):
            for c in range(3):
                inner[level, i - 1, c] = spread(five[c], level, 8)
            for c in range(2):
                side[level, i - 1, c] = spread(five[3 + c], level, 16).astype(BF16)
    odd = lane % 2 == 1
    middle = jnp.where(odd, west, east)
    lower = turn(middle, 2)
    y_low = jnp.where(odd, turn(west, 1), turn(own_right, -1))
    stay, up, down, left, right = five_weights(
        middle[:levels], lower[:levels], middle[levels:], y_low[levels:]
    )
    odd = odd[:levels]
    outer_w = jnp.where(odd, left, right)
    inner_w = jnp.where(odd, right, left)
    lane8 = lanes((8, cells))
    span = cells // levels
    for c, x in enumerate((stay, up, down, outer_w, inner_w)):
        out = jnp.zeros((8, cells), F32)
        for level in range(levels):
            out = jnp.where(lane8 // span == level, turn(spread(x, level, 8), level * span - 4), out)
        edge[c] = out


def place_corners(levels, came, corner_ref):
    padded, cells = corner_ref.shape
    width = 4 * levels
    span = cells // levels
    mine = own_lanes(padded, cells, width)
    parts, picks = [], []
    sub, lane = sublanes((cells, cells)) % width, lanes((cells, cells))
    for n, x in enumerate(came):
        x = jnp.broadcast_to(x.astype(F32)[:, None, :], (padded // 8, 8, cells))
        parts.append(jnp.where(mine, x.reshape(padded, cells), 0.0).astype(BF16))
        target = sub // 4 * span + (1, 0, span - 1, span - 2)[n]
        picks.append(jnp.where((sub % 4 == n) & (lane == target), 1.0, 0.0).astype(BF16))
    both = jnp.dot(
        jnp.concatenate(parts, axis=1), jnp.concatenate(picks, axis=0), preferred_element_type=F32
    )
    corner_ref[...] = both.astype(BF16)


def side_columns(rows, levels, right_ref, left_ref, west_ref, east_ref, edge, mid_ref, corner_ref, next_ref):
    padded, cells = right_ref.shape
    span = cells // levels
    lane = lanes((16, cells))
    odd = lane % 2 == 1
    row_of = (lane % span) // 2

    def group(g, carry):
        part = pl.ds(pl.multiple_of(g * 16, 16), 16)
        lo, hi = west_ref[part, :].astype(F32), east_ref[part, :].astype(F32)
        own_r, own_l = right_ref[part, :].astype(F32), left_ref[part, :].astype(F32)
        corner = corner_ref[part, :].astype(F32)
        weights = [jnp.concatenate([edge[c]] * 2, axis=0) for c in range(5)]
        mid = jnp.where(odd, lo, hi)
        outside = jnp.where(odd, turn(lo, 1), turn(hi, -1))
        inside = jnp.where(odd, turn(own_l, 1), turn(own_r, -1))
        above = jnp.where(row_of == rows - 1, corner, turn(mid, -2))
        below = jnp.where(row_of == 0, corner, turn(mid, 2))
        mid_ref[part, :] = mid.astype(BF16)
        after = (
            weights[0] * mid + weights[1] * above + weights[2] * below
            + weights[3] * outside + weights[4] * inside
        )
        next_ref[part, :] = after.astype(BF16)
        return carry

    lax.fori_loop(0, padded // 16, group, 0, unroll=2)


def gather_fields(came_ref, label_v, label_s, total, beside, sem):
    owners, _, cells = came_ref.shape
    levfields = (came_ref.shape[1] - 32) // CAP
    rows = total.shape[0] // levfields - 1
    tail = CAP * levfields

    def read(d, sums):
        x = came_ref[d, pl.ds(tail, 32), :].astype(F32)
        label_v[pl.ds(d, 1), :] = x[0:1].astype(jnp.int32)
        return sums + x

    beside[...] = lax.fori_loop(0, owners, read, jnp.zeros((32, cells), F32), unroll=4)
    copies = fetch([label_v], [label_s], sem)
    total[...] = jnp.zeros_like(total)
    finish(copies)

    def add(d, carry):
        for k in range(CAP):
            at = pl.multiple_of(label_s[d, 2 * rows + 8 + k] * levfields, 8)
            total[pl.ds(at, levfields), :] += came_ref[d, pl.ds(k * levfields, levfields), :].astype(F32)
        return carry

    lax.fori_loop(0, owners, add, 0, unroll=4)


def light_of(levels, optical):
    depth = softplus(optical)
    parts, running = [], jnp.zeros((1, depth.shape[1]), F32)
    for level in range(levels):
        running = running + depth[level : level + 1]
        parts.append(jnp.exp(-running))
    return jnp.concatenate(parts, axis=0)


def advect_kernel(
    levels, planes_any, below_any, above_any, right_any, left_any, west_any, east_any,
    came_any, rate_any, around_any, out_any, tile_any,
    planes, below_ref, above_ref, right_ref, left_ref, west_ref, east_ref,
    came_ref, rate_ref,
    tile_ref, total, factor, label_v, label_s, ghost,
    inner, side, edge, mid_ref, corner_ref, next_ref, matrix, low_mask, high_mask, once, once16,
    plane_sems, in_sems, out_sems,
):
    levfields, rows, cells = tile_ref.shape
    padded = planes.shape[1]
    species = out_any.shape[0]
    span = cells // levels
    small = fetch(
        [came_any, rate_any, west_any, east_any, right_any, left_any, below_any, above_any],
        [came_ref, rate_ref, west_ref, east_ref, right_ref, left_ref, below_ref, above_ref], in_sems,
    )
    parts = [pl.ds(level * rows, rows) for level in range(levels)]
    fetch([planes_any.at[p] for p in parts], [planes.at[p] for p in parts], plane_sems)
    sub, lane = sublanes((cells, cells)), lanes((cells, cells))
    low_mask[...] = jnp.where(sub == lane - 1, 1.0, 0.0).astype(BF16)
    high_mask[...] = jnp.where(sub == lane + 1, 1.0, 0.0).astype(BF16)
    finish(small[:1])
    gather_fields(came_ref, label_v, label_s, total, ghost, in_sems)
    for fl in range(levfields):
        for r in range(0, rows, 8):
            tile_ref[fl, pl.ds(r, 8), :] = total[pl.ds(r * levfields + fl, 8, stride=levfields), :]
    tile_copy = fetch([tile_ref], [tile_any], in_sems)
    fields = 2 * levels
    ghosts = 0.3 * jnp.tanh(ghost[...])
    line = [ghosts[24:32], ghosts[8:16]]
    for r in range(rows):
        line.append(0.3 * jnp.tanh(total[pl.ds(r * levfields, fields), :]))
        x = total[pl.ds(r * levfields, levfields), :]
        light = light_of(levels, x[fields : fields + levels])
        x = jnp.concatenate([x, light, jnp.zeros((16 - levels, cells), F32)], axis=0)
        high = x.astype(BF16)
        rest = (x - high.astype(F32)).astype(BF16)
        factor[r] = jnp.concatenate([high, rest, high], axis=0)
    line.append(ghosts[16:24])
    make_weights(levels, line, ghosts[0:8], turn(ghosts[0:8], cells // 2), inner, side, edge)
    finish(small[1:])
    packed = padded // 8
    place_corners(levels, [
        ref[pl.ds(padded + n * packed, packed), :] for n in range(2) for ref in (west_ref, east_ref)
    ], corner_ref)
    side_columns(rows, levels, right_ref, left_ref, west_ref, east_ref, edge, mid_ref, corner_ref, next_ref)
    sub16, lane16 = sublanes((16, cells)), lanes((16, cells))

    def set_matrix(level, i):
        left, right = side[level, i + 1, 0], side[level, i + 1, 1]
        for t in range(cells // 16):
            at = pl.ds(16 * t, 16)
            matrix[i + 1, at, :] = low_mask[at, :] * left + high_mask[at, :] * right
        matrix[i + 1, pl.ds(cells, cells), :] = jnp.zeros((cells, cells), BF16)
        p = 2 * min(max(i, 0), rows - 1)
        tile = jnp.where(
            (sub16 == p % 16 + 1) & (lane16 == 0), left.astype(F32),
            jnp.where((sub16 == p % 16) & (lane16 == cells - 1), right.astype(F32), 0.0),
        )
        at = pl.multiple_of(cells + level * span + p // 16 * 16, 16)
        matrix[i + 1, pl.ds(at, 16), :] = tile.astype(BF16)

    def weighted(weights, x, up, down):
        count = x.shape[0] // 8
        stay, up_w, down_w = (w[None] for w in weights)
        x, up, down = (v.reshape(count, 8, cells) for v in (x, up, down))
        return (stay * x + up_w * up + down_w * down).reshape(count * 8, cells)

    def one_level(level, carry):
        part = pl.ds(level * rows, rows)
        pltpu.make_async_copy(planes_any.at[part], planes.at[part], plane_sems.at[level]).wait()
        for i in range(-1, rows + 1):
            set_matrix(level, i)

        def half(b, carry):
            part = pl.ds(pl.multiple_of(b * HALF, HALF), HALF)

            def before(i):
                if i < 0:
                    return below_ref[i + 2, level, part, :].astype(F32)
                if i >= rows:
                    return above_ref[i - rows, level, part, :].astype(F32)
                return planes[level * rows + i, part, :]

            for i in range(-1, rows + 1):
                x = before(i)
                beside = (mid_ref if 0 <= i < rows else corner_ref)[part, :]
                both = jnp.concatenate([x.astype(BF16), beside], axis=1)
                across = jnp.dot(both, matrix[i + 1], preferred_element_type=F32)
                weights = [inner[level, i + 1, c] for c in range(3)]
                x = weighted(weights, x, before(i + 1), before(i - 1)) + across
                once[i + 1] = x
                if 0 <= i < rows:
                    once16[i] = x.astype(BF16)
            for i in range(rows):
                both = jnp.concatenate([once16[i], next_ref[part, :]], axis=1)
                across = jnp.dot(both, matrix[i + 1], preferred_element_type=F32)
                weights = [inner[level, i + 1, c] for c in range(3)]
                moved = weighted(weights, once[i + 1], once[i + 2], once[i]) + across
                exponent = jnp.dot(rate_ref[level, part, :], factor[i], preferred_element_type=F32)
                planes[level * rows + i, part, :] = moved * pl.reciprocal(
                    1.0 + softplus(exponent), approx=False
                )
            return carry

        lax.fori_loop(0, padded // HALF, half, 0)
        for r in range(rows):
            k = level * rows + r
            pltpu.make_async_copy(
                planes.at[k, pl.ds(0, species), :], out_any.at[:, k, 0, :], out_sems.at[k]
            ).start()
        return carry

    lax.fori_loop(0, levels, one_level, 0)
    finish(tile_copy)
    for k in range(levels * rows):
        pltpu.make_async_copy(
            planes.at[k, pl.ds(0, species), :], out_any.at[:, k, 0, :], out_sems.at[k]
        ).wait()


def advect(planes, below, above, right, left, west, east, came, rate, around, species):
    levels, padded, cells = below.shape[1:]
    count = planes.shape[0]
    rows = count // levels
    owners = came.shape[0]
    levfields = (came.shape[1] - 32) // CAP
    tile = jax.ShapeDtypeStruct((levfields, rows, cells), F32)
    small = [below, above, right, left, west, east, came, rate]
    column = pltpu.VMEM((padded, cells), BF16)
    square = pltpu.VMEM((cells, cells), BF16)
    return pl.pallas_call(
        functools.partial(advect_kernel, levels),
        out_shape=(jax.ShapeDtypeStruct((species, count, 1, cells), F32), tile),
        in_specs=here(2 + len(small)),
        out_specs=tuple(here(2)),
        scratch_shapes=[
            pltpu.VMEM((count, padded, cells), F32),
            *buffers(small), *buffers([tile]),
            pltpu.VMEM(((rows + 1) * levfields, cells), F32),
            pltpu.VMEM((rows, rate.shape[2], cells), BF16),
            pltpu.VMEM((owners, cells), jnp.int32), pltpu.SMEM((owners, cells), jnp.int32),
            pltpu.VMEM((32, cells), F32),
            pltpu.VMEM((levels, rows + 2, 3, 8, cells), F32),
            pltpu.VMEM((levels, rows + 2, 2, 16, cells), BF16),
            pltpu.VMEM((5, 8, cells), F32),
            column, column, column,
            pltpu.VMEM((rows + 2, 2 * cells, cells), BF16),
            square, square,
            pltpu.VMEM((rows + 2, HALF, cells), F32),
            pltpu.VMEM((rows, HALF, cells), BF16),
            pltpu.SemaphoreType.DMA((levels,)), pltpu.SemaphoreType.DMA((len(small),)),
            pltpu.SemaphoreType.DMA((count,)),
        ],
        compiler_params=params(ADV),
        cost_estimate=pl.CostEstimate(
            flops=60 * planes.size, bytes_accessed=8 * planes.size, transcendentals=3 * planes.size
        ),
        name="advect",
    )(planes, *small, around)


def arrived_kernel(*refs):
    refs[-1][...] = jnp.zeros_like(refs[-1])


def arrived(arrays):
    return pl.pallas_call(
        arrived_kernel,
        out_shape=jax.ShapeDtypeStruct((8, 128), F32),
        in_specs=here(len(arrays)),
        compiler_params=params(1),
        cost_estimate=pl.CostEstimate(flops=MIB, bytes_accessed=0, transcendentals=0),
        name="arrived",
    )(*arrays)


def rate_factors(rate_coef, photo_coef, levels, padded):
    species, fields = rate_coef.shape
    same = jnp.eye(levels, dtype=F32)
    by_field = rate_coef[None, :, :, None] * same[:, None, None, :]
    by_light = photo_coef[None, :, None] * same[:, None, :]
    table = jnp.concatenate([by_field.reshape(levels, species, fields * levels), by_light], axis=2)
    table = jnp.pad(table, ((0, 0), (0, padded - species), (0, 64 - table.shape[2])))
    high = lax.reduce_precision(table, 8, 7)
    rest = (table - high).astype(BF16)
    high = high.astype(BF16)
    return jnp.concatenate([high, high, rest], axis=2)


def shift(x, axis, by):
    count = lax.axis_size(axis)
    return lax.ppermute(x, axis, [(i, (i + by) % count) for i in range(count)])


def local(met_src, intersection_weights, block_dest, block_row, tracers, rate_coef, photo_coef):
    n_face, n_tile = lax.axis_size("face"), lax.axis_size("tile")
    species, levels, rows, cells = tracers.shape
    padded = -(-species // HALF) * HALF
    tracer_planes = tracers.reshape(species, levels * rows, 1, cells)

    payload = regrid(block_dest, block_row, met_src, intersection_weights, n_face, n_tile, rows)
    payload, tracer_planes = lax.optimization_barrier((payload, tracer_planes))
    came = lax.all_to_all(payload, ("face", "tile"), split_axis=0, concat_axis=0, tiled=True)

    top, bottom, corner = border_rows(tracer_planes, padded, levels, rows)
    corner_below = shift(corner, "face", 1)
    corner_above = shift(corner, "face", -1)
    below = shift(bottom, "face", 1)
    above = shift(top, "face", -1)
    tracer_planes, top, bottom = lax.optimization_barrier((tracer_planes, top, bottom))
    planes, right, left = columns(tracer_planes, padded, levels)
    west = shift(jnp.concatenate([right, corner_below, corner_above], axis=0), "tile", 1)
    east = shift(jnp.concatenate([left, corner_below, corner_above], axis=0), "tile", -1)
    beside = arrived([west, east])
    around = arrived([below, above, beside])
    rate = rate_factors(rate_coef, photo_coef, levels, padded)
    out, met_tile = advect(planes, below, above, right, left, west, east, came, rate, around, species)
    fields = rate_coef.shape[1]
    return met_tile.reshape(fields, levels, rows, cells), out.reshape(species, levels, rows, cells)


def solution(mesh):
    return jax.shard_map(
        local,
        mesh=mesh,
        in_specs=(
            P(("face", "tile"), None, None),
            P(("face", "tile"), None, None),
            P(("face", "tile")),
            P(("face", "tile")),
            P(None, None, "face", "tile"),
            P(),
            P(),
        ),
        out_specs=(P(None, None, "face", "tile"), P(None, None, "face", "tile")),
        check_vma=False,
    )
```

```python
import functools

import jax
import jax.numpy as jnp
from jax import lax
from jax.experimental import pallas as pl
from jax.experimental.pallas import tpu as pltpu
from jax.sharding import PartitionSpec as P

CAP = 2
F32 = jnp.float32
BF16 = jnp.bfloat16
HALF = 256
COL = 50
BIG = 50
ADV = 50
BIGGEST = 60
MIB = 1024 * 1024
SMEM = pltpu.MemorySpace.SMEM
VMEM = pltpu.MemorySpace.VMEM


def here(count):
    return [pl.BlockSpec(memory_space=pl.ANY)] * count


def params(mib):
    return pltpu.CompilerParams(vmem_limit_bytes=mib * MIB)


def buffers(arrays):
    return [pltpu.VMEM(x.shape, x.dtype) for x in arrays]


def fetch(sources, targets, sems):
    copies = [pltpu.make_async_copy(s, t, sems.at[i]) for i, (s, t) in enumerate(zip(sources, targets))]
    for copy in copies:
        copy.start()
    return copies


def finish(copies):
    for copy in copies:
        copy.wait()


def lanes(shape):
    return lax.broadcasted_iota(jnp.int32, shape, len(shape) - 1)


def sublanes(shape):
    return lax.broadcasted_iota(jnp.int32, shape, len(shape) - 2)


def turn(x, shift):
    count = x.shape[-1]
    shift = shift % count
    return x if shift == 0 else pltpu.roll(x, shift, x.ndim - 1)


def regrid_kernel(n_tile, rows, dest_any, row_any, src_any, weight_any, out_any,
                  dest_ref, row_ref, src_ref, weight_ref, out_ref, line_ref, column_ref, index_ref, count_ref, sems):
    owners = out_ref.shape[0]
    n_face = owners // n_tile
    blocks, levfields, cells = src_ref.shape
    copies = fetch([dest_any, row_any, src_any, weight_any], [dest_ref, row_ref, src_ref, weight_ref], sems)

    def clear(d, carry):
        count_ref[d] = 0
        for k in range(CAP):
            index_ref[d * CAP + k] = -1
        return carry

    lax.fori_loop(0, owners, clear, 0, unroll=8)
    finish(copies[:2])

    def place(b, carry):
        d = dest_ref[b]
        k = count_ref[d]
        index_ref[d * CAP + jnp.minimum(k, CAP - 1)] = b
        count_ref[d] = k + 1
        return carry

    lax.fori_loop(0, blocks, place, 0, unroll=8)
    finish(copies[2:])
    lane = lanes((8, cells))
    pair = lane // 2
    half = cells // 2
    tail = CAP * levfields

    def product(d, carry):
        zero = jnp.zeros((8, cells), F32)
        west, east, line = zero, zero, [zero, zero, zero]
        labels = zero
        for k in range(CAP):
            b = index_ref[d * CAP + k]
            used = b >= 0
            at = jnp.maximum(b, 0)
            x = jnp.dot(src_ref[at], weight_ref[at], preferred_element_type=F32)
            x = jnp.where(used, x, 0.0).astype(BF16)
            out_ref[d, pl.ds(k * levfields, levfields), :] = x
            head = x[0:16].astype(F32)[0:8]
            row = jnp.where(used, row_ref[at], rows)
            moved = pltpu.roll(head, jnp.mod(2 * row + 6, cells), 1)
            west += jnp.where(pair == row + 2, moved, 0.0)
            east += jnp.where(pair == row + 3, moved, 0.0)
            for n, r in enumerate((rows - 1, 0, rows - 2)):
                line[n] += jnp.where(row == r, head, 0.0)
            labels = jnp.where(lane == 2 * rows + 8 + k, row.astype(F32), labels)
        column = jnp.where(lane < half, west, 0.0) + turn(east, half - 2)
        column_ref[d, 0] = column
        column_ref[d, 1] = turn(column, -2 * rows)
        column_ref[d, 2] = turn(column, 2 * rows)
        column_ref[d, 3] = labels
        for n in range(3):
            line_ref[d, n] = line[n]
        return carry

    slots, around = pl.ds(0, tail), pl.ds(tail, 32)
    copies = []
    for h in range(2):
        first, last = h * owners // 2, (h + 1) * owners // 2
        lax.fori_loop(first, last, product, 0, unroll=16)
        part = pl.ds(first, last - first)
        copies += fetch([out_ref.at[part, slots, :]], [out_any.at[part, slots, :]], sems.at[pl.ds(h, 1)])
    inside = lane % half
    in_rows = (inside >= 4) & (inside < 4 + 2 * rows)
    before = (inside >= 2) & (inside < 4)
    after = (inside >= 4 + 2 * rows) & (inside < 6 + 2 * rows)
    is_west = lane < half

    def surround(d, carry):
        f, t = d // n_tile, d % n_tile
        up, down = jnp.where(f == 0, n_face - 1, f - 1), jnp.where(f == n_face - 1, 0, f + 1)
        low, high = jnp.where(t == 0, n_tile - 1, t - 1), jnp.where(t == n_tile - 1, 0, t + 1)
        tile = column_ref[d, 3]
        for side, x in ((is_west, low), (~is_west, high)):
            tile += jnp.where(side & in_rows, column_ref[f * n_tile + x, 0], 0.0)
            tile += jnp.where(side & before, column_ref[up * n_tile + x, 1], 0.0)
            tile += jnp.where(side & after, column_ref[down * n_tile + x, 2], 0.0)
        parts = [tile, line_ref[up * n_tile + t, 0], line_ref[down * n_tile + t, 1], line_ref[up * n_tile + t, 2]]
        out_ref[d, pl.ds(tail, 32), :] = jnp.concatenate(parts, axis=0).astype(BF16)
        return carry

    lax.fori_loop(0, owners, surround, 0, unroll=8)
    finish(copies + fetch([out_ref.at[:, around, :]], [out_any.at[:, around, :]], sems.at[pl.ds(2, 1)]))


def regrid(block_dest, block_row, met_src, weights, n_face, n_tile, rows):
    blocks, levfields, cells = met_src.shape
    owners = n_face * n_tile
    out = jax.ShapeDtypeStruct((owners, CAP * levfields + 32, cells), BF16)
    return pl.pallas_call(
        functools.partial(regrid_kernel, n_tile, rows),
        out_shape=out,
        in_specs=here(4),
        out_specs=here(1)[0],
        scratch_shapes=[
            pltpu.SMEM(block_dest.shape, jnp.int32), pltpu.SMEM(block_row.shape, jnp.int32),
            *buffers([met_src, weights, out]),
            pltpu.VMEM((owners, 3, 8, cells), F32), pltpu.VMEM((owners, 4, 8, cells), F32),
            pltpu.SMEM((owners * CAP,), jnp.int32), pltpu.SMEM((owners,), jnp.int32),
            pltpu.SemaphoreType.DMA((4,)),
        ],
        compiler_params=params(BIGGEST),
        cost_estimate=pl.CostEstimate(
            flops=2 * blocks * levfields * cells * cells, bytes_accessed=6 * MIB, transcendentals=0
        ),
        name="regrid",
    )(block_dest, block_row, met_src, weights)


def own_lanes(padded, cells, width):
    shape = (padded, cells)
    return lanes(shape) // width == sublanes(shape) % 8


def row_kernel(rows, tracer_any, top_any, bottom_any, corner_any, border, top_ref, bottom_ref, corner_ref, sems):
    levels, padded, cells = top_ref.shape[1:]
    species = tracer_any.shape[0]
    width = 4 * levels
    sub, lane = sublanes((cells, cells)), lanes((cells, cells)) % width
    column = jnp.where(lane % 2 == 0, cells - 1, 0)
    spread_out = jnp.zeros((padded, cells), F32)
    wanted = [(level, row) for level in range(levels) for row in (0, 1, rows - 2, rows - 1)]
    finish(fetch(
        [tracer_any.at[:, level * rows + row, 0, :] for level, row in wanted],
        [border.at[i, pl.ds(0, species), :] for i in range(len(wanted))], sems,
    ))
    for i, (level, row) in enumerate(wanted):
        x = border[i].astype(BF16)
        if row < 2:
            top_ref[row, level] = x
        else:
            bottom_ref[row - rows + 2, level] = x
        if row in (0, rows - 1):
            from_row = lane // 2 == 2 * level + (1 if row == 0 else 0)
            select = jnp.where((sub == column) & from_row, 1.0, 0.0).astype(BF16)
            spread_out += jnp.dot(x, select, preferred_element_type=F32)
    packed = jnp.where(own_lanes(padded, cells, width), spread_out, 0.0)
    corner_ref[...] = jnp.sum(packed.reshape(padded // 8, 8, cells), axis=1).astype(BF16)
    finish(fetch([top_ref, bottom_ref, corner_ref], [top_any, bottom_any, corner_any], sems))


def border_rows(planes, padded, levels, rows):
    cells = planes.shape[3]
    line = jax.ShapeDtypeStruct((2, levels, padded, cells), BF16)
    corner = jax.ShapeDtypeStruct((padded // 8, cells), BF16)
    return pl.pallas_call(
        functools.partial(row_kernel, rows),
        out_shape=(line, line, corner),
        in_specs=here(1),
        out_specs=tuple(here(3)),
        scratch_shapes=[
            pltpu.VMEM((4 * levels, padded, cells), F32), *buffers([line, line, corner]),
            pltpu.SemaphoreType.DMA((4 * levels,)),
        ],
        compiler_params=params(BIG),
        cost_estimate=pl.CostEstimate(flops=planes.size, bytes_accessed=planes.size, transcendentals=0),
        name="border_rows",
    )(planes)


def load_planes(source, target, sems):
    species = source.shape[0]
    copies = []
    for k in range(source.shape[1]):
        copy = pltpu.make_async_copy(source.at[:, k, 0, :], target.at[k, pl.ds(0, species), :], sems.at[k])
        copy.start()
        copies.append(copy)
    return copies


def column_kernel(levels, tracer_any, planes_any, right_ref, left_ref, planes, total, picker, sems, out_sems):
    count, padded, cells = planes.shape
    rows = count // levels
    load_planes(tracer_any, planes, sems)
    total[...] = jnp.zeros_like(total)
    picker[...] = jnp.zeros_like(picker)
    sub, lane = sublanes((16, 2 * cells)), lanes((16, 2 * cells))

    def one_level(level, carry):
        for row in range(rows):
            pltpu.make_async_copy(
                tracer_any.at[:, level * rows + row, 0, :],
                planes.at[level * rows + row, pl.ds(0, tracer_any.shape[0]), :],
                sems.at[level * rows + row],
            ).wait()
        part = pl.ds(level * rows, rows)
        pltpu.make_async_copy(planes.at[part], planes_any.at[part], out_sems.at[level]).start()
        for row in range(0, rows, 2):
            pair = []
            for h in range(2):
                k = level * rows + row + h
                pair.append(planes[k].astype(BF16))
                low = (sub < 2) & (lane == cells + 2 * k + sub)
                high = (sub >= 14) & (lane == 2 * k + sub - 14)
                picker[row // 2, pl.ds(h * cells, 16), :] = jnp.where(low, 1.0, 0.0).astype(BF16)
                picker[row // 2, pl.ds((h + 1) * cells - 16, 16), :] = jnp.where(high, 1.0, 0.0).astype(BF16)
            both = jnp.concatenate(pair, axis=1)
            total[...] += jnp.dot(both, picker[row // 2], preferred_element_type=F32)
        return carry

    lax.fori_loop(0, levels, one_level, 0)
    for level in range(levels):
        part = pl.ds(level * rows, rows)
        pltpu.make_async_copy(planes.at[part], planes_any.at[part], out_sems.at[level]).wait()
    right_ref[...] = total[:, 0:cells].astype(BF16)
    left_ref[...] = total[:, cells:].astype(BF16)


def columns(planes, padded, levels):
    _, count, _, cells = planes.shape
    side = jax.ShapeDtypeStruct((padded, cells), BF16)
    return pl.pallas_call(
        functools.partial(column_kernel, levels),
        out_shape=(
            jax.ShapeDtypeStruct((count, padded, cells), F32), side, side,
        ),
        in_specs=here(1),
        out_specs=(*here(1), *[pl.BlockSpec(memory_space=VMEM)] * 2),
        scratch_shapes=[
            pltpu.VMEM((count, padded, cells), F32),
            pltpu.VMEM((padded, 2 * cells), F32), pltpu.VMEM((count // levels // 2, 2 * cells, 2 * cells), BF16),
            pltpu.SemaphoreType.DMA((count,)), pltpu.SemaphoreType.DMA((levels,)),
        ],
        compiler_params=params(COL),
        cost_estimate=pl.CostEstimate(flops=12 * planes.size, bytes_accessed=4 * planes.size, transcendentals=0),
        name="columns",
    )(planes)


def softplus(x):
    return jnp.maximum(x, jnp.log(1.0 + jnp.exp(jnp.minimum(x, 60.0))))


def five_weights(face_x, face_x_low, face_y, face_y_low):
    up = -jnp.minimum(face_x, 0.0)
    down = jnp.maximum(face_x_low, 0.0)
    right = -jnp.minimum(face_y, 0.0)
    left = jnp.maximum(face_y_low, 0.0)
    stay = (
        1.0
        - (jnp.maximum(face_x, 0.0) - jnp.minimum(face_x_low, 0.0))
        - (jnp.maximum(face_y, 0.0) - jnp.minimum(face_y_low, 0.0))
    )
    return stay, up, down, left, right


def spread(x, level, count):
    return jnp.broadcast_to(x[level : level + 1], (count, x.shape[1]))


def make_weights(levels, line, west, east, inner, side, edge):
    rows = len(line) - 3
    fields, cells = line[0].shape
    lane = lanes((fields, cells))
    own_right = jnp.zeros((fields, cells), F32)
    for i in range(2, rows + 2):
        own_right = jnp.where(lane // 2 == i, turn(line[i], 2 * i - (cells - 2)), own_right)
    for i in range(1, rows + 3):
        now, low = line[i], line[i - 1]
        face_y_low = jnp.where(lane == 0, turn(west, -(2 * i + 1)), turn(now, 1))[levels:]
        five = five_weights(now[:levels], low[:levels], now[levels:], face_y_low)
        for level in range(levels):
            for c in range(3):
                inner[level, i - 1, c] = spread(five[c], level, 8)
            for c in range(2):
                side[level, i - 1, c] = spread(five[3 + c], level, 16).astype(BF16)
    odd = lane % 2 == 1
    middle = jnp.where(odd, west, east)
    lower = turn(middle, 2)
    y_low = jnp.where(odd, turn(west, 1), turn(own_right, -1))
    stay, up, down, left, right = five_weights(
        middle[:levels], lower[:levels], middle[levels:], y_low[levels:]
    )
    odd = odd[:levels]
    outer_w = jnp.where(odd, left, right)
    inner_w = jnp.where(odd, right, left)
    lane8 = lanes((8, cells))
    span = cells // levels
    for c, x in enumerate((stay, up, down, outer_w, inner_w)):
        out = jnp.zeros((8, cells), F32)
        for level in range(levels):
            out = jnp.where(lane8 // span == level, turn(spread(x, level, 8), level * span - 4), out)
        edge[c] = out


def place_corners(levels, came, corner_ref):
    padded, cells = corner_ref.shape
    width = 4 * levels
    span = cells // levels
    mine = own_lanes(padded, cells, width)
    parts, picks = [], []
    sub, lane = sublanes((cells, cells)) % width, lanes((cells, cells))
    for n, x in enumerate(came):
        x = jnp.broadcast_to(x.astype(F32)[:, None, :], (padded // 8, 8, cells))
        parts.append(jnp.where(mine, x.reshape(padded, cells), 0.0).astype(BF16))
        target = sub // 4 * span + (1, 0, span - 1, span - 2)[n]
        picks.append(jnp.where((sub % 4 == n) & (lane == target), 1.0, 0.0).astype(BF16))
    both = jnp.dot(
        jnp.concatenate(parts, axis=1), jnp.concatenate(picks, axis=0), preferred_element_type=F32
    )
    corner_ref[...] = both.astype(BF16)


def side_columns(rows, levels, right_ref, left_ref, west_ref, east_ref, edge, mid_ref, corner_ref, next_ref):
    padded, cells = right_ref.shape
    span = cells // levels
    lane = lanes((16, cells))
    odd = lane % 2 == 1
    row_of = (lane % span) // 2

    def group(g, carry):
        part = pl.ds(pl.multiple_of(g * 16, 16), 16)
        lo, hi = west_ref[part, :].astype(F32), east_ref[part, :].astype(F32)
        own_r, own_l = right_ref[part, :].astype(F32), left_ref[part, :].astype(F32)
        corner = corner_ref[part, :].astype(F32)
        weights = [jnp.concatenate([edge[c]] * 2, axis=0) for c in range(5)]
        mid = jnp.where(odd, lo, hi)
        outside = jnp.where(odd, turn(lo, 1), turn(hi, -1))
        inside = jnp.where(odd, turn(own_l, 1), turn(own_r, -1))
        above = jnp.where(row_of == rows - 1, corner, turn(mid, -2))
        below = jnp.where(row_of == 0, corner, turn(mid, 2))
        mid_ref[part, :] = mid.astype(BF16)
        after = (
            weights[0] * mid + weights[1] * above + weights[2] * below
            + weights[3] * outside + weights[4] * inside
        )
        next_ref[part, :] = after.astype(BF16)
        return carry

    lax.fori_loop(0, padded // 16, group, 0, unroll=2)


def read_labels(came_ref, label_v, beside):
    owners, _, cells = came_ref.shape
    tail = came_ref.shape[1] - 32

    def read(d, sums):
        x = came_ref[d, pl.ds(tail, 32), :].astype(F32)
        label_v[pl.ds(d, 1), :] = x[0:1].astype(jnp.int32)
        return sums + x

    beside[...] = lax.fori_loop(0, owners, read, jnp.zeros((32, cells), F32), unroll=8)


def add_slots(came_ref, label_s, total):
    owners = came_ref.shape[0]
    levfields = (came_ref.shape[1] - 32) // CAP
    rows = total.shape[0] // levfields - 1

    def add(d, carry):
        for k in range(CAP):
            at = pl.multiple_of(label_s[d, 2 * rows + 8 + k] * levfields, 8)
            total[pl.ds(at, levfields), :] += came_ref[d, pl.ds(k * levfields, levfields), :].astype(F32)
        return carry

    lax.fori_loop(0, owners, add, 0, unroll=4)


def light_of(levels, optical):
    depth = softplus(optical)
    parts, running = [], jnp.zeros((1, depth.shape[1]), F32)
    for level in range(levels):
        running = running + depth[level : level + 1]
        parts.append(jnp.exp(-running))
    return jnp.concatenate(parts, axis=0)


def advect_kernel(
    levels, planes_any, below_any, above_any, right_any, left_any, west_any, east_any,
    came_any, rate_any, around_any, out_any, tile_any,
    planes, below_ref, above_ref, right_ref, left_ref, west_ref, east_ref,
    came_ref, rate_ref,
    tile_ref, total, factor, label_v, label_s, ghost,
    inner, side, edge, mid_ref, corner_ref, next_ref, matrix, low_mask, high_mask, once, once16,
    plane_sems, in_sems, out_sems,
):
    levfields, rows, cells = tile_ref.shape
    padded = planes.shape[1]
    species = out_any.shape[0]
    span = cells // levels
    small = fetch(
        [came_any, rate_any, west_any, east_any, right_any, left_any, below_any, above_any],
        [came_ref, rate_ref, west_ref, east_ref, right_ref, left_ref, below_ref, above_ref], in_sems,
    )
    parts = [pl.ds(level * rows, rows) for level in range(levels)]
    sub, lane = sublanes((cells, cells)), lanes((cells, cells))
    finish(small[:1])
    fetch([planes_any.at[p] for p in parts], [planes.at[p] for p in parts], plane_sems)
    read_labels(came_ref, label_v, ghost)
    label_copy = fetch([label_v], [label_s], in_sems)
    total[...] = jnp.zeros_like(total)
    low_mask[...] = jnp.where(sub == lane - 1, 1.0, 0.0).astype(BF16)
    high_mask[...] = jnp.where(sub == lane + 1, 1.0, 0.0).astype(BF16)
    finish(small[1:])
    packed = padded // 8
    place_corners(levels, [
        ref[pl.ds(padded + n * packed, packed), :] for n in range(2) for ref in (west_ref, east_ref)
    ], corner_ref)
    finish(label_copy)
    add_slots(came_ref, label_s, total)
    for fl in range(levfields):
        for r in range(0, rows, 8):
            tile_ref[fl, pl.ds(r, 8), :] = total[pl.ds(r * levfields + fl, 8, stride=levfields), :]
    tile_copy = fetch([tile_ref], [tile_any], in_sems)
    fields = 2 * levels
    ghosts = 0.3 * jnp.tanh(ghost[...])
    line = [ghosts[24:32], ghosts[8:16]]
    for r in range(rows):
        line.append(0.3 * jnp.tanh(total[pl.ds(r * levfields, fields), :]))
        x = total[pl.ds(r * levfields, levfields), :]
        light = light_of(levels, x[fields : fields + levels])
        x = jnp.concatenate([x, light, jnp.zeros((16 - levels, cells), F32)], axis=0)
        high = x.astype(BF16)
        rest = (x - high.astype(F32)).astype(BF16)
        factor[r // 2, :, pl.ds(r % 2 * cells, cells)] = jnp.concatenate([high, rest, high], axis=0)
    line.append(ghosts[16:24])
    make_weights(levels, line, ghosts[0:8], turn(ghosts[0:8], cells // 2), inner, side, edge)
    side_columns(rows, levels, right_ref, left_ref, west_ref, east_ref, edge, mid_ref, corner_ref, next_ref)
    sub16, lane16 = sublanes((16, cells)), lanes((16, cells))

    def set_matrix(level, i):
        left, right = side[level, i + 1, 0], side[level, i + 1, 1]
        for t in range(cells // 16):
            at = pl.ds(16 * t, 16)
            matrix[i + 1, at, :] = low_mask[at, :] * left + high_mask[at, :] * right
        matrix[i + 1, pl.ds(cells, cells), :] = jnp.zeros((cells, cells), BF16)
        p = 2 * min(max(i, 0), rows - 1)
        tile = jnp.where(
            (sub16 == p % 16 + 1) & (lane16 == 0), left.astype(F32),
            jnp.where((sub16 == p % 16) & (lane16 == cells - 1), right.astype(F32), 0.0),
        )
        at = pl.multiple_of(cells + level * span + p // 16 * 16, 16)
        matrix[i + 1, pl.ds(at, 16), :] = tile.astype(BF16)

    def weighted(weights, x, up, down):
        count = x.shape[0] // 8
        stay, up_w, down_w = (w[None] for w in weights)
        x, up, down = (v.reshape(count, 8, cells) for v in (x, up, down))
        return (stay * x + up_w * up + down_w * down).reshape(count * 8, cells)

    def send(level, first, last):
        for r in range(first, last):
            k = level * rows + r
            pltpu.make_async_copy(
                planes.at[k, pl.ds(0, species), :], out_any.at[:, k, 0, :], out_sems.at[k]
            ).start()

    def one_level(level, carry):
        part = pl.ds(level * rows, rows)
        pltpu.make_async_copy(planes_any.at[part], planes.at[part], plane_sems.at[level]).wait()
        for i in range(-1, rows + 1):
            set_matrix(level, i)

        def half(b, carry):
            part = pl.ds(pl.multiple_of(b * HALF, HALF), HALF)

            def before(i):
                if i < 0:
                    return below_ref[i + 2, level, part, :].astype(F32)
                if i >= rows:
                    return above_ref[i - rows, level, part, :].astype(F32)
                return planes[level * rows + i, part, :]

            beside_next = next_ref[part, :]
            for i in range(-1, rows + 1):
                x = before(i)
                beside = (mid_ref if 0 <= i < rows else corner_ref)[part, :]
                both = jnp.concatenate([x.astype(BF16), beside], axis=1)
                across = jnp.dot(both, matrix[i + 1], preferred_element_type=F32)
                weights = [inner[level, i + 1, c] for c in range(3)]
                x = weighted(weights, x, before(i + 1), before(i - 1)) + across
                once[i + 1] = x
                if 0 <= i < rows:
                    once16[i] = x.astype(BF16)
            for i in range(rows):
                both = jnp.concatenate([once16[i], beside_next], axis=1)
                across = jnp.dot(both, matrix[i + 1], preferred_element_type=F32)
                weights = [inner[level, i + 1, c] for c in range(3)]
                moved = weighted(weights, once[i + 1], once[i + 2], once[i]) + across
                if i % 2 == 0:
                    exponents = jnp.dot(rate_ref[level, part, :], factor[i // 2], preferred_element_type=F32)
                exponent = exponents[:, i % 2 * cells : (i % 2 + 1) * cells]
                planes[level * rows + i, part, :] = moved * pl.reciprocal(
                    1.0 + softplus(exponent), approx=False
                )
                if i == rows // 2 and HALF == padded:
                    send(level, 0, rows // 2)
            return carry

        lax.fori_loop(0, padded // HALF, half, 0)
        send(level, rows // 2 if HALF == padded else 0, rows)
        return carry

    lax.fori_loop(0, levels, one_level, 0)
    finish(tile_copy)
    for k in range(levels * rows):
        pltpu.make_async_copy(
            planes.at[k, pl.ds(0, species), :], out_any.at[:, k, 0, :], out_sems.at[k]
        ).wait()


def advect(planes, below, above, right, left, west, east, came, rate, around, species):
    levels, padded, cells = below.shape[1:]
    count = planes.shape[0]
    rows = count // levels
    owners = came.shape[0]
    levfields = (came.shape[1] - 32) // CAP
    tile = jax.ShapeDtypeStruct((levfields, rows, cells), F32)
    small = [below, above, right, left, west, east, came, rate]
    column = pltpu.VMEM((padded, cells), BF16)
    square = pltpu.VMEM((cells, cells), BF16)
    return pl.pallas_call(
        functools.partial(advect_kernel, levels),
        out_shape=(jax.ShapeDtypeStruct((species, count, 1, cells), F32), tile),
        in_specs=here(2 + len(small)),
        out_specs=tuple(here(2)),
        scratch_shapes=[
            pltpu.VMEM((count, padded, cells), F32),
            *buffers(small), *buffers([tile]),
            pltpu.VMEM(((rows + 1) * levfields, cells), F32),
            pltpu.VMEM((rows // 2, rate.shape[2], 2 * cells), BF16),
            pltpu.VMEM((owners, cells), jnp.int32), pltpu.SMEM((owners, cells), jnp.int32),
            pltpu.VMEM((32, cells), F32),
            pltpu.VMEM((levels, rows + 2, 3, 8, cells), F32),
            pltpu.VMEM((levels, rows + 2, 2, 16, cells), BF16),
            pltpu.VMEM((5, 8, cells), F32),
            column, column, column,
            pltpu.VMEM((rows + 2, 2 * cells, cells), BF16),
            square, square,
            pltpu.VMEM((rows + 2, HALF, cells), F32),
            pltpu.VMEM((rows, HALF, cells), BF16),
            pltpu.SemaphoreType.DMA((levels,)), pltpu.SemaphoreType.DMA((len(small),)),
            pltpu.SemaphoreType.DMA((count,)),
        ],
        compiler_params=params(ADV),
        cost_estimate=pl.CostEstimate(
            flops=60 * planes.size, bytes_accessed=8 * planes.size, transcendentals=3 * planes.size
        ),
        name="advect",
    )(planes, *small, around)


def arrived_kernel(*refs):
    refs[-1][...] = jnp.zeros_like(refs[-1])


def arrived(arrays):
    return pl.pallas_call(
        arrived_kernel,
        out_shape=jax.ShapeDtypeStruct((8, 128), F32),
        in_specs=here(len(arrays)),
        compiler_params=params(1),
        cost_estimate=pl.CostEstimate(flops=MIB, bytes_accessed=0, transcendentals=0),
        name="arrived",
    )(*arrays)


def rate_factors(rate_coef, photo_coef, levels, padded):
    species, fields = rate_coef.shape
    same = jnp.eye(levels, dtype=F32)
    by_field = rate_coef[None, :, :, None] * same[:, None, None, :]
    by_light = photo_coef[None, :, None] * same[:, None, :]
    table = jnp.concatenate([by_field.reshape(levels, species, fields * levels), by_light], axis=2)
    table = jnp.pad(table, ((0, 0), (0, padded - species), (0, 64 - table.shape[2])))
    high = lax.reduce_precision(table, 8, 7)
    rest = (table - high).astype(BF16)
    high = high.astype(BF16)
    return jnp.concatenate([high, high, rest], axis=2)


def shift(x, axis, by):
    count = lax.axis_size(axis)
    return lax.ppermute(x, axis, [(i, (i + by) % count) for i in range(count)])


def local(met_src, intersection_weights, block_dest, block_row, tracers, rate_coef, photo_coef):
    n_face, n_tile = lax.axis_size("face"), lax.axis_size("tile")
    species, levels, rows, cells = tracers.shape
    padded = -(-species // HALF) * HALF
    tracer_planes = tracers.reshape(species, levels * rows, 1, cells)

    payload = regrid(block_dest, block_row, met_src, intersection_weights, n_face, n_tile, rows)
    payload, tracer_planes = lax.optimization_barrier((payload, tracer_planes))
    came = lax.all_to_all(payload, ("face", "tile"), split_axis=0, concat_axis=0, tiled=True)

    top, bottom, corner = border_rows(tracer_planes, padded, levels, rows)
    corner_below = shift(corner, "face", 1)
    corner_above = shift(corner, "face", -1)
    below = shift(bottom, "face", 1)
    above = shift(top, "face", -1)
    tracer_planes, top, bottom = lax.optimization_barrier((tracer_planes, top, bottom))
    planes, right, left = columns(tracer_planes, padded, levels)
    west = shift(jnp.concatenate([right, corner_below, corner_above], axis=0), "tile", 1)
    east = shift(jnp.concatenate([left, corner_below, corner_above], axis=0), "tile", -1)
    beside = arrived([west, east])
    around = arrived([below, above, beside])
    rate = rate_factors(rate_coef, photo_coef, levels, padded)
    out, met_tile = advect(planes, below, above, right, left, west, east, came, rate, around, species)
    fields = rate_coef.shape[1]
    return met_tile.reshape(fields, levels, rows, cells), out.reshape(species, levels, rows, cells)


def solution(mesh):
    return jax.shard_map(
        local,
        mesh=mesh,
        in_specs=(
            P(("face", "tile"), None, None),
            P(("face", "tile"), None, None),
            P(("face", "tile")),
            P(("face", "tile")),
            P(None, None, "face", "tile"),
            P(),
            P(),
        ),
        out_specs=(P(None, None, "face", "tile"), P(None, None, "face", "tile")),
        check_vma=False,
    )
```

```python
import functools

import jax
import jax.numpy as jnp
from jax import lax
from jax.experimental import pallas as pl
from jax.experimental.pallas import tpu as pltpu
from jax.sharding import PartitionSpec as P

CAP = 2
F32 = jnp.float32
BF16 = jnp.bfloat16
HALF = 256
COL = 50
BIG = 50
ADV = 50
BIGGEST = 60
MIB = 1024 * 1024
SMEM = pltpu.MemorySpace.SMEM
VMEM = pltpu.MemorySpace.VMEM


def here(count):
    return [pl.BlockSpec(memory_space=pl.ANY)] * count


def params(mib):
    return pltpu.CompilerParams(vmem_limit_bytes=mib * MIB)


def buffers(arrays):
    return [pltpu.VMEM(x.shape, x.dtype) for x in arrays]


def fetch(sources, targets, sems):
    copies = [pltpu.make_async_copy(s, t, sems.at[i]) for i, (s, t) in enumerate(zip(sources, targets))]
    for copy in copies:
        copy.start()
    return copies


def finish(copies):
    for copy in copies:
        copy.wait()


def lanes(shape):
    return lax.broadcasted_iota(jnp.int32, shape, len(shape) - 1)


def sublanes(shape):
    return lax.broadcasted_iota(jnp.int32, shape, len(shape) - 2)


def turn(x, shift):
    count = x.shape[-1]
    shift = shift % count
    return x if shift == 0 else pltpu.roll(x, shift, x.ndim - 1)


def regrid_kernel(n_tile, rows, dest_any, row_any, src_any, weight_any, out_any,
                  dest_ref, row_ref, src_ref, weight_ref, out_ref, line_ref, column_ref, index_ref, count_ref, sems):
    owners = out_ref.shape[0]
    n_face = owners // n_tile
    blocks, levfields, cells = src_ref.shape
    copies = fetch([dest_any, row_any, src_any, weight_any], [dest_ref, row_ref, src_ref, weight_ref], sems)

    def clear(d, carry):
        count_ref[d] = 0
        for k in range(CAP):
            index_ref[d * CAP + k] = -1
        return carry

    lax.fori_loop(0, owners, clear, 0, unroll=8)
    finish(copies[:2])

    def place(b, carry):
        d = dest_ref[b]
        k = count_ref[d]
        index_ref[d * CAP + jnp.minimum(k, CAP - 1)] = b
        count_ref[d] = k + 1
        return carry

    lax.fori_loop(0, blocks, place, 0, unroll=8)
    finish(copies[2:])
    lane = lanes((8, cells))
    pair = lane // 2
    half = cells // 2
    tail = CAP * levfields

    def product(d, carry):
        zero = jnp.zeros((8, cells), F32)
        west, east, line = zero, zero, [zero, zero, zero]
        labels = zero
        for k in range(CAP):
            b = index_ref[d * CAP + k]
            used = b >= 0
            at = jnp.maximum(b, 0)
            x = jnp.dot(src_ref[at], weight_ref[at], preferred_element_type=F32)
            x = jnp.where(used, x, 0.0).astype(BF16)
            out_ref[d, pl.ds(k * levfields, levfields), :] = x
            head = x[0:16].astype(F32)[0:8]
            row = jnp.where(used, row_ref[at], rows)
            moved = pltpu.roll(head, jnp.mod(2 * row + 6, cells), 1)
            west += jnp.where(pair == row + 2, moved, 0.0)
            east += jnp.where(pair == row + 3, moved, 0.0)
            for n, r in enumerate((rows - 1, 0, rows - 2)):
                line[n] += jnp.where(row == r, head, 0.0)
            labels = jnp.where(lane == 2 * rows + 8 + k, row.astype(F32), labels)
        column = jnp.where(lane < half, west, 0.0) + turn(east, half - 2)
        column_ref[d, 0] = column
        column_ref[d, 1] = turn(column, -2 * rows)
        column_ref[d, 2] = turn(column, 2 * rows)
        column_ref[d, 3] = labels
        for n in range(3):
            line_ref[d, n] = line[n]
        return carry

    slots, around = pl.ds(0, tail), pl.ds(tail, 32)
    copies = []
    for h in range(2):
        first, last = h * owners // 2, (h + 1) * owners // 2
        lax.fori_loop(first, last, product, 0, unroll=16)
        part = pl.ds(first, last - first)
        copies += fetch([out_ref.at[part, slots, :]], [out_any.at[part, slots, :]], sems.at[pl.ds(h, 1)])
    inside = lane % half
    in_rows = (inside >= 4) & (inside < 4 + 2 * rows)
    before = (inside >= 2) & (inside < 4)
    after = (inside >= 4 + 2 * rows) & (inside < 6 + 2 * rows)
    is_west = lane < half

    def surround(d, carry):
        f, t = d // n_tile, d % n_tile
        up, down = jnp.where(f == 0, n_face - 1, f - 1), jnp.where(f == n_face - 1, 0, f + 1)
        low, high = jnp.where(t == 0, n_tile - 1, t - 1), jnp.where(t == n_tile - 1, 0, t + 1)
        tile = column_ref[d, 3]
        for side, x in ((is_west, low), (~is_west, high)):
            tile += jnp.where(side & in_rows, column_ref[f * n_tile + x, 0], 0.0)
            tile += jnp.where(side & before, column_ref[up * n_tile + x, 1], 0.0)
            tile += jnp.where(side & after, column_ref[down * n_tile + x, 2], 0.0)
        parts = [tile, line_ref[up * n_tile + t, 0], line_ref[down * n_tile + t, 1], line_ref[up * n_tile + t, 2]]
        out_ref[d, pl.ds(tail, 32), :] = jnp.concatenate(parts, axis=0).astype(BF16)
        return carry

    lax.fori_loop(0, owners, surround, 0, unroll=8)
    finish(copies + fetch([out_ref.at[:, around, :]], [out_any.at[:, around, :]], sems.at[pl.ds(2, 1)]))


def regrid(block_dest, block_row, met_src, weights, n_face, n_tile, rows):
    blocks, levfields, cells = met_src.shape
    owners = n_face * n_tile
    out = jax.ShapeDtypeStruct((owners, CAP * levfields + 32, cells), BF16)
    return pl.pallas_call(
        functools.partial(regrid_kernel, n_tile, rows),
        out_shape=out,
        in_specs=here(4),
        out_specs=here(1)[0],
        scratch_shapes=[
            pltpu.SMEM(block_dest.shape, jnp.int32), pltpu.SMEM(block_row.shape, jnp.int32),
            *buffers([met_src, weights, out]),
            pltpu.VMEM((owners, 3, 8, cells), F32), pltpu.VMEM((owners, 4, 8, cells), F32),
            pltpu.SMEM((owners * CAP,), jnp.int32), pltpu.SMEM((owners,), jnp.int32),
            pltpu.SemaphoreType.DMA((4,)),
        ],
        compiler_params=params(BIGGEST),
        cost_estimate=pl.CostEstimate(
            flops=2 * blocks * levfields * cells * cells, bytes_accessed=6 * MIB, transcendentals=0
        ),
        name="regrid",
    )(block_dest, block_row, met_src, weights)


def own_lanes(padded, cells, width):
    shape = (padded, cells)
    return lanes(shape) // width == sublanes(shape) % 8


def row_kernel(rows, tracer_any, top_any, bottom_any, corner_any, border, top_ref, bottom_ref, corner_ref, sems):
    levels, padded, cells = top_ref.shape[1:]
    species = tracer_any.shape[0]
    width = 4 * levels
    sub, lane = sublanes((cells, cells)), lanes((cells, cells)) % width
    column = jnp.where(lane % 2 == 0, cells - 1, 0)
    spread_out = jnp.zeros((padded, cells), F32)
    wanted = [(level, row) for level in range(levels) for row in (0, 1, rows - 2, rows - 1)]
    finish(fetch(
        [tracer_any.at[:, level * rows + row, 0, :] for level, row in wanted],
        [border.at[i, pl.ds(0, species), :] for i in range(len(wanted))], sems,
    ))
    for i, (level, row) in enumerate(wanted):
        x = border[i].astype(BF16)
        if row < 2:
            top_ref[row, level] = x
        else:
            bottom_ref[row - rows + 2, level] = x
        if row in (0, rows - 1):
            from_row = lane // 2 == 2 * level + (1 if row == 0 else 0)
            select = jnp.where((sub == column) & from_row, 1.0, 0.0).astype(BF16)
            spread_out += jnp.dot(x, select, preferred_element_type=F32)
    packed = jnp.where(own_lanes(padded, cells, width), spread_out, 0.0)
    corner_ref[...] = jnp.sum(packed.reshape(padded // 8, 8, cells), axis=1).astype(BF16)
    finish(fetch([top_ref, bottom_ref, corner_ref], [top_any, bottom_any, corner_any], sems))


def border_rows(planes, padded, levels, rows):
    cells = planes.shape[3]
    line = jax.ShapeDtypeStruct((2, levels, padded, cells), BF16)
    corner = jax.ShapeDtypeStruct((padded // 8, cells), BF16)
    return pl.pallas_call(
        functools.partial(row_kernel, rows),
        out_shape=(line, line, corner),
        in_specs=here(1),
        out_specs=tuple(here(3)),
        scratch_shapes=[
            pltpu.VMEM((4 * levels, padded, cells), F32), *buffers([line, line, corner]),
            pltpu.SemaphoreType.DMA((4 * levels,)),
        ],
        compiler_params=params(BIG),
        cost_estimate=pl.CostEstimate(flops=planes.size, bytes_accessed=planes.size, transcendentals=0),
        name="border_rows",
    )(planes)


def load_planes(source, target, sems):
    species = source.shape[0]
    copies = []
    for k in range(source.shape[1]):
        copy = pltpu.make_async_copy(source.at[:, k, 0, :], target.at[k, pl.ds(0, species), :], sems.at[k])
        copy.start()
        copies.append(copy)
    return copies


def column_kernel(levels, tracer_any, planes_any, right_ref, left_ref, planes, total, picker, sems, out_sems):
    count, padded, cells = planes.shape
    rows = count // levels
    load_planes(tracer_any, planes, sems)
    total[...] = jnp.zeros_like(total)
    picker[...] = jnp.zeros_like(picker)
    sub, lane = sublanes((16, 2 * cells)), lanes((16, 2 * cells))

    def one_level(level, carry):
        for row in range(rows):
            pltpu.make_async_copy(
                tracer_any.at[:, level * rows + row, 0, :],
                planes.at[level * rows + row, pl.ds(0, tracer_any.shape[0]), :],
                sems.at[level * rows + row],
            ).wait()
        part = pl.ds(level * rows, rows)
        pltpu.make_async_copy(planes.at[part], planes_any.at[part], out_sems.at[level]).start()
        for row in range(0, rows, 2):
            pair = []
            for h in range(2):
                k = level * rows + row + h
                pair.append(planes[k].astype(BF16))
                low = (sub < 2) & (lane == cells + 2 * k + sub)
                high = (sub >= 14) & (lane == 2 * k + sub - 14)
                picker[row // 2, pl.ds(h * cells, 16), :] = jnp.where(low, 1.0, 0.0).astype(BF16)
                picker[row // 2, pl.ds((h + 1) * cells - 16, 16), :] = jnp.where(high, 1.0, 0.0).astype(BF16)
            both = jnp.concatenate(pair, axis=1)
            total[...] += jnp.dot(both, picker[row // 2], preferred_element_type=F32)
        return carry

    lax.fori_loop(0, levels, one_level, 0)
    for level in range(levels):
        part = pl.ds(level * rows, rows)
        pltpu.make_async_copy(planes.at[part], planes_any.at[part], out_sems.at[level]).wait()
    right_ref[...] = total[:, 0:cells].astype(BF16)
    left_ref[...] = total[:, cells:].astype(BF16)


def columns(planes, padded, levels):
    _, count, _, cells = planes.shape
    side = jax.ShapeDtypeStruct((padded, cells), BF16)
    return pl.pallas_call(
        functools.partial(column_kernel, levels),
        out_shape=(
            jax.ShapeDtypeStruct((count, padded, cells), F32), side, side,
        ),
        in_specs=here(1),
        out_specs=(*here(1), *[pl.BlockSpec(memory_space=VMEM)] * 2),
        scratch_shapes=[
            pltpu.VMEM((count, padded, cells), F32),
            pltpu.VMEM((padded, 2 * cells), F32), pltpu.VMEM((count // levels // 2, 2 * cells, 2 * cells), BF16),
            pltpu.SemaphoreType.DMA((count,)), pltpu.SemaphoreType.DMA((levels,)),
        ],
        compiler_params=params(COL),
        cost_estimate=pl.CostEstimate(flops=12 * planes.size, bytes_accessed=4 * planes.size, transcendentals=0),
        name="columns",
    )(planes)


def softplus(x):
    return jnp.maximum(x, jnp.log(1.0 + jnp.exp(jnp.minimum(x, 60.0))))


def five_weights(face_x, face_x_low, face_y, face_y_low):
    up = -jnp.minimum(face_x, 0.0)
    down = jnp.maximum(face_x_low, 0.0)
    right = -jnp.minimum(face_y, 0.0)
    left = jnp.maximum(face_y_low, 0.0)
    stay = (
        1.0
        - (jnp.maximum(face_x, 0.0) - jnp.minimum(face_x_low, 0.0))
        - (jnp.maximum(face_y, 0.0) - jnp.minimum(face_y_low, 0.0))
    )
    return stay, up, down, left, right


def spread(x, level, count):
    return jnp.broadcast_to(x[level : level + 1], (count, x.shape[1]))


def make_weights(levels, line, west, east, inner, side, edge):
    rows = len(line) - 3
    fields, cells = line[0].shape
    lane = lanes((fields, cells))
    own_right = jnp.zeros((fields, cells), F32)
    for i in range(2, rows + 2):
        own_right = jnp.where(lane // 2 == i, turn(line[i], 2 * i - (cells - 2)), own_right)
    for i in range(1, rows + 3):
        now, low = line[i], line[i - 1]
        face_y_low = jnp.where(lane == 0, turn(west, -(2 * i + 1)), turn(now, 1))[levels:]
        five = five_weights(now[:levels], low[:levels], now[levels:], face_y_low)
        for level in range(levels):
            for c in range(3):
                inner[level, i - 1, c] = spread(five[c], level, 8)
            for c in range(2):
                side[level, i - 1, c] = spread(five[3 + c], level, 16).astype(BF16)
    odd = lane % 2 == 1
    middle = jnp.where(odd, west, east)
    lower = turn(middle, 2)
    y_low = jnp.where(odd, turn(west, 1), turn(own_right, -1))
    stay, up, down, left, right = five_weights(
        middle[:levels], lower[:levels], middle[levels:], y_low[levels:]
    )
    odd = odd[:levels]
    outer_w = jnp.where(odd, left, right)
    inner_w = jnp.where(odd, right, left)
    lane8 = lanes((8, cells))
    span = cells // levels
    for c, x in enumerate((stay, up, down, outer_w, inner_w)):
        out = jnp.zeros((8, cells), F32)
        for level in range(levels):
            out = jnp.where(lane8 // span == level, turn(spread(x, level, 8), level * span - 4), out)
        edge[c] = out


def place_corners(levels, came, corner_ref):
    padded, cells = corner_ref.shape
    width = 4 * levels
    span = cells // levels
    mine = own_lanes(padded, cells, width)
    parts, picks = [], []
    sub, lane = sublanes((cells, cells)) % width, lanes((cells, cells))
    for n, x in enumerate(came):
        x = jnp.broadcast_to(x.astype(F32)[:, None, :], (padded // 8, 8, cells))
        parts.append(jnp.where(mine, x.reshape(padded, cells), 0.0).astype(BF16))
        target = sub // 4 * span + (1, 0, span - 1, span - 2)[n]
        picks.append(jnp.where((sub % 4 == n) & (lane == target), 1.0, 0.0).astype(BF16))
    both = jnp.dot(
        jnp.concatenate(parts, axis=1), jnp.concatenate(picks, axis=0), preferred_element_type=F32
    )
    corner_ref[...] = both.astype(BF16)


def side_columns(rows, levels, right_ref, left_ref, west_ref, east_ref, edge, mid_ref, corner_ref, next_ref):
    padded, cells = right_ref.shape
    span = cells // levels
    lane = lanes((16, cells))
    odd = lane % 2 == 1
    row_of = (lane % span) // 2

    def group(g, carry):
        part = pl.ds(pl.multiple_of(g * 16, 16), 16)
        lo, hi = west_ref[part, :].astype(F32), east_ref[part, :].astype(F32)
        own_r, own_l = right_ref[part, :].astype(F32), left_ref[part, :].astype(F32)
        corner = corner_ref[part, :].astype(F32)
        weights = [jnp.concatenate([edge[c]] * 2, axis=0) for c in range(5)]
        mid = jnp.where(odd, lo, hi)
        outside = jnp.where(odd, turn(lo, 1), turn(hi, -1))
        inside = jnp.where(odd, turn(own_l, 1), turn(own_r, -1))
        above = jnp.where(row_of == rows - 1, corner, turn(mid, -2))
        below = jnp.where(row_of == 0, corner, turn(mid, 2))
        mid_ref[part, :] = mid.astype(BF16)
        after = (
            weights[0] * mid + weights[1] * above + weights[2] * below
            + weights[3] * outside + weights[4] * inside
        )
        next_ref[part, :] = after.astype(BF16)
        return carry

    lax.fori_loop(0, padded // 16, group, 0, unroll=8)


def read_labels(came_ref, label_v, beside):
    owners, _, cells = came_ref.shape
    tail = came_ref.shape[1] - 32

    def read(d, sums):
        x = came_ref[d, pl.ds(tail, 32), :].astype(F32)
        label_v[pl.ds(d, 1), :] = x[0:1].astype(jnp.int32)
        return sums + x

    beside[...] = lax.fori_loop(0, owners, read, jnp.zeros((32, cells), F32), unroll=16)


def add_slots(came_ref, label_s, total):
    owners = came_ref.shape[0]
    levfields = (came_ref.shape[1] - 32) // CAP
    rows = total.shape[0] // levfields - 1

    def add(d, carry):
        for k in range(CAP):
            at = pl.multiple_of(label_s[d, 2 * rows + 8 + k] * levfields, 8)
            total[pl.ds(at, levfields), :] += came_ref[d, pl.ds(k * levfields, levfields), :].astype(F32)
        return carry

    lax.fori_loop(0, owners, add, 0, unroll=16)


def light_of(levels, optical):
    depth = softplus(optical)
    parts, running = [], jnp.zeros((1, depth.shape[1]), F32)
    for level in range(levels):
        running = running + depth[level : level + 1]
        parts.append(jnp.exp(-running))
    return jnp.concatenate(parts, axis=0)


def advect_kernel(
    levels, planes_any, below_any, above_any, right_any, left_any, west_any, east_any,
    came_any, rate_any, around_any, out_any, tile_any,
    planes, below_ref, above_ref, right_ref, left_ref, west_ref, east_ref,
    came_ref, rate_ref,
    tile_ref, total, factor, label_v, label_s, ghost,
    inner, side, edge, mid_ref, corner_ref, next_ref, matrix, low_mask, high_mask, once, once16,
    plane_sems, in_sems, out_sems,
):
    levfields, rows, cells = tile_ref.shape
    padded = planes.shape[1]
    species = out_any.shape[0]
    span = cells // levels
    small = fetch(
        [came_any, rate_any, west_any, east_any, right_any, left_any, below_any, above_any],
        [came_ref, rate_ref, west_ref, east_ref, right_ref, left_ref, below_ref, above_ref], in_sems,
    )
    parts = [pl.ds(level * rows, rows) for level in range(levels)]
    sub, lane = sublanes((cells, cells)), lanes((cells, cells))
    finish(small[:1])
    fetch([planes_any.at[p] for p in parts], [planes.at[p] for p in parts], plane_sems)
    read_labels(came_ref, label_v, ghost)
    label_copy = fetch([label_v], [label_s], in_sems)
    total[...] = jnp.zeros_like(total)
    low_mask[...] = jnp.where(sub == lane - 1, 1.0, 0.0).astype(BF16)
    high_mask[...] = jnp.where(sub == lane + 1, 1.0, 0.0).astype(BF16)
    finish(small[1:])
    packed = padded // 8
    place_corners(levels, [
        ref[pl.ds(padded + n * packed, packed), :] for n in range(2) for ref in (west_ref, east_ref)
    ], corner_ref)
    finish(label_copy)
    add_slots(came_ref, label_s, total)
    for fl in range(levfields):
        for r in range(0, rows, 8):
            tile_ref[fl, pl.ds(r, 8), :] = total[pl.ds(r * levfields + fl, 8, stride=levfields), :]
    tile_copy = fetch([tile_ref], [tile_any], in_sems)
    fields = 2 * levels
    ghosts = 0.3 * jnp.tanh(ghost[...])
    line = [ghosts[24:32], ghosts[8:16]]
    for r in range(rows):
        line.append(0.3 * jnp.tanh(total[pl.ds(r * levfields, fields), :]))
        x = total[pl.ds(r * levfields, levfields), :]
        light = light_of(levels, x[fields : fields + levels])
        x = jnp.concatenate([x, light, jnp.zeros((16 - levels, cells), F32)], axis=0)
        high = x.astype(BF16)
        rest = (x - high.astype(F32)).astype(BF16)
        factor[r // 2, :, pl.ds(r % 2 * cells, cells)] = jnp.concatenate([high, rest, high], axis=0)
    line.append(ghosts[16:24])
    make_weights(levels, line, ghosts[0:8], turn(ghosts[0:8], cells // 2), inner, side, edge)
    side_columns(rows, levels, right_ref, left_ref, west_ref, east_ref, edge, mid_ref, corner_ref, next_ref)
    sub16, lane16 = sublanes((16, cells)), lanes((16, cells))

    def set_matrix(level, i):
        left, right = side[level, i + 1, 0], side[level, i + 1, 1]
        for t in range(cells // 16):
            at = pl.ds(16 * t, 16)
            matrix[i + 1, at, :] = low_mask[at, :] * left + high_mask[at, :] * right
        matrix[i + 1, pl.ds(cells, cells), :] = jnp.zeros((cells, cells), BF16)
        p = 2 * min(max(i, 0), rows - 1)
        tile = jnp.where(
            (sub16 == p % 16 + 1) & (lane16 == 0), left.astype(F32),
            jnp.where((sub16 == p % 16) & (lane16 == cells - 1), right.astype(F32), 0.0),
        )
        at = pl.multiple_of(cells + level * span + p // 16 * 16, 16)
        matrix[i + 1, pl.ds(at, 16), :] = tile.astype(BF16)

    def weighted(weights, x, up, down):
        count = x.shape[0] // 8
        stay, up_w, down_w = (w[None] for w in weights)
        x, up, down = (v.reshape(count, 8, cells) for v in (x, up, down))
        return (stay * x + up_w * up + down_w * down).reshape(count * 8, cells)

    def send(level, first, last):
        for r in range(first, last):
            k = level * rows + r
            pltpu.make_async_copy(
                planes.at[k, pl.ds(0, species), :], out_any.at[:, k, 0, :], out_sems.at[k]
            ).start()

    def one_level(level, carry):
        part = pl.ds(level * rows, rows)
        pltpu.make_async_copy(planes_any.at[part], planes.at[part], plane_sems.at[level]).wait()
        for i in range(-1, rows + 1):
            set_matrix(level, i)

        def half(b, carry):
            part = pl.ds(pl.multiple_of(b * HALF, HALF), HALF)

            def before(i):
                if i < 0:
                    return below_ref[i + 2, level, part, :].astype(F32)
                if i >= rows:
                    return above_ref[i - rows, level, part, :].astype(F32)
                return planes[level * rows + i, part, :]

            beside_next = next_ref[part, :]
            for i in range(-1, rows + 1):
                x = before(i)
                beside = (mid_ref if 0 <= i < rows else corner_ref)[part, :]
                both = jnp.concatenate([x.astype(BF16), beside], axis=1)
                across = jnp.dot(both, matrix[i + 1], preferred_element_type=F32)
                weights = [inner[level, i + 1, c] for c in range(3)]
                x = weighted(weights, x, before(i + 1), before(i - 1)) + across
                once[i + 1] = x
                if 0 <= i < rows:
                    once16[i] = x.astype(BF16)
            for i in range(rows):
                both = jnp.concatenate([once16[i], beside_next], axis=1)
                across = jnp.dot(both, matrix[i + 1], preferred_element_type=F32)
                weights = [inner[level, i + 1, c] for c in range(3)]
                moved = weighted(weights, once[i + 1], once[i + 2], once[i]) + across
                if i % 2 == 0:
                    exponents = jnp.dot(rate_ref[level, part, :], factor[i // 2], preferred_element_type=F32)
                exponent = exponents[:, i % 2 * cells : (i % 2 + 1) * cells]
                planes[level * rows + i, part, :] = moved * pl.reciprocal(
                    1.0 + softplus(exponent), approx=False
                )
                if i == rows // 2 and HALF == padded:
                    send(level, 0, rows // 2)
            return carry

        lax.fori_loop(0, padded // HALF, half, 0)
        send(level, rows // 2 if HALF == padded else 0, rows)
        return carry

    lax.fori_loop(0, levels, one_level, 0)
    finish(tile_copy)
    for k in range(levels * rows):
        pltpu.make_async_copy(
            planes.at[k, pl.ds(0, species), :], out_any.at[:, k, 0, :], out_sems.at[k]
        ).wait()


def advect(planes, below, above, right, left, west, east, came, rate, around, species):
    levels, padded, cells = below.shape[1:]
    count = planes.shape[0]
    rows = count // levels
    owners = came.shape[0]
    levfields = (came.shape[1] - 32) // CAP
    tile = jax.ShapeDtypeStruct((levfields, rows, cells), F32)
    small = [below, above, right, left, west, east, came, rate]
    column = pltpu.VMEM((padded, cells), BF16)
    square = pltpu.VMEM((cells, cells), BF16)
    return pl.pallas_call(
        functools.partial(advect_kernel, levels),
        out_shape=(jax.ShapeDtypeStruct((species, count, 1, cells), F32), tile),
        in_specs=here(2 + len(small)),
        out_specs=tuple(here(2)),
        scratch_shapes=[
            pltpu.VMEM((count, padded, cells), F32),
            *buffers(small), *buffers([tile]),
            pltpu.VMEM(((rows + 1) * levfields, cells), F32),
            pltpu.VMEM((rows // 2, rate.shape[2], 2 * cells), BF16),
            pltpu.VMEM((owners, cells), jnp.int32), pltpu.SMEM((owners, cells), jnp.int32),
            pltpu.VMEM((32, cells), F32),
            pltpu.VMEM((levels, rows + 2, 3, 8, cells), F32),
            pltpu.VMEM((levels, rows + 2, 2, 16, cells), BF16),
            pltpu.VMEM((5, 8, cells), F32),
            column, column, column,
            pltpu.VMEM((rows + 2, 2 * cells, cells), BF16),
            square, square,
            pltpu.VMEM((rows + 2, HALF, cells), F32),
            pltpu.VMEM((rows, HALF, cells), BF16),
            pltpu.SemaphoreType.DMA((levels,)), pltpu.SemaphoreType.DMA((len(small),)),
            pltpu.SemaphoreType.DMA((count,)),
        ],
        compiler_params=params(ADV),
        cost_estimate=pl.CostEstimate(
            flops=60 * planes.size, bytes_accessed=8 * planes.size, transcendentals=3 * planes.size
        ),
        name="advect",
    )(planes, *small, around)


def arrived_kernel(*refs):
    refs[-1][...] = jnp.zeros_like(refs[-1])


def arrived(arrays):
    return pl.pallas_call(
        arrived_kernel,
        out_shape=jax.ShapeDtypeStruct((8, 128), F32),
        in_specs=here(len(arrays)),
        compiler_params=params(1),
        cost_estimate=pl.CostEstimate(flops=MIB, bytes_accessed=0, transcendentals=0),
        name="arrived",
    )(*arrays)


def rate_factors(rate_coef, photo_coef, levels, padded):
    species, fields = rate_coef.shape
    same = jnp.eye(levels, dtype=F32)
    by_field = rate_coef[None, :, :, None] * same[:, None, None, :]
    by_light = photo_coef[None, :, None] * same[:, None, :]
    table = jnp.concatenate([by_field.reshape(levels, species, fields * levels), by_light], axis=2)
    table = jnp.pad(table, ((0, 0), (0, padded - species), (0, 64 - table.shape[2])))
    high = lax.reduce_precision(table, 8, 7)
    rest = (table - high).astype(BF16)
    high = high.astype(BF16)
    return jnp.concatenate([high, high, rest], axis=2)


def shift(x, axis, by):
    count = lax.axis_size(axis)
    return lax.ppermute(x, axis, [(i, (i + by) % count) for i in range(count)])


def local(met_src, intersection_weights, block_dest, block_row, tracers, rate_coef, photo_coef):
    n_face, n_tile = lax.axis_size("face"), lax.axis_size("tile")
    species, levels, rows, cells = tracers.shape
    padded = -(-species // HALF) * HALF
    tracer_planes = tracers.reshape(species, levels * rows, 1, cells)

    payload = regrid(block_dest, block_row, met_src, intersection_weights, n_face, n_tile, rows)
    payload, tracer_planes = lax.optimization_barrier((payload, tracer_planes))
    came = lax.all_to_all(payload, ("face", "tile"), split_axis=0, concat_axis=0, tiled=True)

    top, bottom, corner = border_rows(tracer_planes, padded, levels, rows)
    corner_below = shift(corner, "face", 1)
    corner_above = shift(corner, "face", -1)
    below = shift(bottom, "face", 1)
    above = shift(top, "face", -1)
    tracer_planes, top, bottom = lax.optimization_barrier((tracer_planes, top, bottom))
    planes, right, left = columns(tracer_planes, padded, levels)
    west = shift(jnp.concatenate([right, corner_below, corner_above], axis=0), "tile", 1)
    east = shift(jnp.concatenate([left, corner_below, corner_above], axis=0), "tile", -1)
    beside = arrived([west, east])
    around = arrived([below, above, beside])
    rate = rate_factors(rate_coef, photo_coef, levels, padded)
    out, met_tile = advect(planes, below, above, right, left, west, east, came, rate, around, species)
    fields = rate_coef.shape[1]
    return met_tile.reshape(fields, levels, rows, cells), out.reshape(species, levels, rows, cells)


def solution(mesh):
    return jax.shard_map(
        local,
        mesh=mesh,
        in_specs=(
            P(("face", "tile"), None, None),
            P(("face", "tile"), None, None),
            P(("face", "tile")),
            P(("face", "tile")),
            P(None, None, "face", "tile"),
            P(),
            P(),
        ),
        out_specs=(P(None, None, "face", "tile"), P(None, None, "face", "tile")),
        check_vma=False,
    )
```

```python
import functools

import jax
import jax.numpy as jnp
from jax import lax
from jax.experimental import pallas as pl
from jax.experimental.pallas import tpu as pltpu
from jax.sharding import PartitionSpec as P

CAP = 2
F32 = jnp.float32
BF16 = jnp.bfloat16
HALF = 256
COL = 50
BIG = 50
ADV = 50
BIGGEST = 60
MIB = 1024 * 1024
SMEM = pltpu.MemorySpace.SMEM
VMEM = pltpu.MemorySpace.VMEM


def here(count):
    return [pl.BlockSpec(memory_space=pl.ANY)] * count


def params(mib):
    return pltpu.CompilerParams(vmem_limit_bytes=mib * MIB)


def buffers(arrays):
    return [pltpu.VMEM(x.shape, x.dtype) for x in arrays]


def fetch(sources, targets, sems):
    copies = [pltpu.make_async_copy(s, t, sems.at[i]) for i, (s, t) in enumerate(zip(sources, targets))]
    for copy in copies:
        copy.start()
    return copies


def finish(copies):
    for copy in copies:
        copy.wait()


def lanes(shape):
    return lax.broadcasted_iota(jnp.int32, shape, len(shape) - 1)


def sublanes(shape):
    return lax.broadcasted_iota(jnp.int32, shape, len(shape) - 2)


def turn(x, shift):
    count = x.shape[-1]
    shift = shift % count
    return x if shift == 0 else pltpu.roll(x, shift, x.ndim - 1)


def regrid_kernel(n_tile, rows, dest_any, row_any, src_any, weight_any, out_any,
                  dest_ref, row_ref, src_ref, weight_ref, out_ref, line_ref, column_ref, index_ref, count_ref, sems):
    owners = out_ref.shape[0]
    n_face = owners // n_tile
    blocks, levfields, cells = src_ref.shape
    copies = fetch([dest_any, row_any, src_any, weight_any], [dest_ref, row_ref, src_ref, weight_ref], sems)

    def clear(d, carry):
        count_ref[d] = 0
        for k in range(CAP):
            index_ref[d * CAP + k] = -1
        return carry

    lax.fori_loop(0, owners, clear, 0, unroll=8)
    finish(copies[:2])

    def place(b, carry):
        d = dest_ref[b]
        k = count_ref[d]
        index_ref[d * CAP + jnp.minimum(k, CAP - 1)] = b
        count_ref[d] = k + 1
        return carry

    lax.fori_loop(0, blocks, place, 0, unroll=8)
    finish(copies[2:])
    lane = lanes((8, cells))
    pair = lane // 2
    half = cells // 2
    tail = CAP * levfields

    def product(d, carry):
        zero = jnp.zeros((8, cells), F32)
        west, east, line = zero, zero, [zero, zero, zero]
        labels = zero
        for k in range(CAP):
            b = index_ref[d * CAP + k]
            used = b >= 0
            at = jnp.maximum(b, 0)
            x = jnp.dot(src_ref[at], weight_ref[at], preferred_element_type=F32)
            x = jnp.where(used, x, 0.0).astype(BF16)
            out_ref[d, pl.ds(k * levfields, levfields), :] = x
            head = x[0:16].astype(F32)[0:8]
            row = jnp.where(used, row_ref[at], rows)
            moved = pltpu.roll(head, jnp.mod(2 * row + 6, cells), 1)
            west += jnp.where(pair == row + 2, moved, 0.0)
            east += jnp.where(pair == row + 3, moved, 0.0)
            for n, r in enumerate((rows - 1, 0, rows - 2)):
                line[n] += jnp.where(row == r, head, 0.0)
            labels = jnp.where(lane == 2 * rows + 8 + k, row.astype(F32), labels)
        column = jnp.where(lane < half, west, 0.0) + turn(east, half - 2)
        column_ref[d, 0] = column
        column_ref[d, 1] = turn(column, -2 * rows)
        column_ref[d, 2] = turn(column, 2 * rows)
        column_ref[d, 3] = labels
        for n in range(3):
            line_ref[d, n] = line[n]
        return carry

    slots, around = pl.ds(0, tail), pl.ds(tail, 32)
    copies = []
    for h in range(2):
        first, last = h * owners // 2, (h + 1) * owners // 2
        lax.fori_loop(first, last, product, 0, unroll=16)
        part = pl.ds(first, last - first)
        copies += fetch([out_ref.at[part, slots, :]], [out_any.at[part, slots, :]], sems.at[pl.ds(h, 1)])
    inside = lane % half
    in_rows = (inside >= 4) & (inside < 4 + 2 * rows)
    before = (inside >= 2) & (inside < 4)
    after = (inside >= 4 + 2 * rows) & (inside < 6 + 2 * rows)
    is_west = lane < half

    def surround(d, carry):
        f, t = d // n_tile, d % n_tile
        up, down = jnp.where(f == 0, n_face - 1, f - 1), jnp.where(f == n_face - 1, 0, f + 1)
        low, high = jnp.where(t == 0, n_tile - 1, t - 1), jnp.where(t == n_tile - 1, 0, t + 1)
        tile = column_ref[d, 3]
        for side, x in ((is_west, low), (~is_west, high)):
            tile += jnp.where(side & in_rows, column_ref[f * n_tile + x, 0], 0.0)
            tile += jnp.where(side & before, column_ref[up * n_tile + x, 1], 0.0)
            tile += jnp.where(side & after, column_ref[down * n_tile + x, 2], 0.0)
        parts = [tile, line_ref[up * n_tile + t, 0], line_ref[down * n_tile + t, 1], line_ref[up * n_tile + t, 2]]
        out_ref[d, pl.ds(tail, 32), :] = jnp.concatenate(parts, axis=0).astype(BF16)
        return carry

    lax.fori_loop(0, owners, surround, 0, unroll=8)
    finish(copies + fetch([out_ref.at[:, around, :]], [out_any.at[:, around, :]], sems.at[pl.ds(2, 1)]))


def regrid(block_dest, block_row, met_src, weights, n_face, n_tile, rows):
    blocks, levfields, cells = met_src.shape
    owners = n_face * n_tile
    out = jax.ShapeDtypeStruct((owners, CAP * levfields + 32, cells), BF16)
    return pl.pallas_call(
        functools.partial(regrid_kernel, n_tile, rows),
        out_shape=out,
        in_specs=here(4),
        out_specs=here(1)[0],
        scratch_shapes=[
            pltpu.SMEM(block_dest.shape, jnp.int32), pltpu.SMEM(block_row.shape, jnp.int32),
            *buffers([met_src, weights, out]),
            pltpu.VMEM((owners, 3, 8, cells), F32), pltpu.VMEM((owners, 4, 8, cells), F32),
            pltpu.SMEM((owners * CAP,), jnp.int32), pltpu.SMEM((owners,), jnp.int32),
            pltpu.SemaphoreType.DMA((4,)),
        ],
        compiler_params=params(BIGGEST),
        cost_estimate=pl.CostEstimate(
            flops=2 * blocks * levfields * cells * cells, bytes_accessed=6 * MIB, transcendentals=0
        ),
        name="regrid",
    )(block_dest, block_row, met_src, weights)


def own_lanes(padded, cells, width):
    shape = (padded, cells)
    return lanes(shape) // width == sublanes(shape) % 8


def row_kernel(rows, tracer_any, top_any, bottom_any, corner_any, border, top_ref, bottom_ref, corner_ref, sems):
    levels, padded, cells = top_ref.shape[1:]
    species = tracer_any.shape[0]
    width = 4 * levels
    sub, lane = sublanes((cells, cells)), lanes((cells, cells)) % width
    column = jnp.where(lane % 2 == 0, cells - 1, 0)
    spread_out = jnp.zeros((padded, cells), F32)
    wanted = [(level, row) for level in range(levels) for row in (0, 1, rows - 2, rows - 1)]
    finish(fetch(
        [tracer_any.at[:, level * rows + row, 0, :] for level, row in wanted],
        [border.at[i, pl.ds(0, species), :] for i in range(len(wanted))], sems,
    ))
    for i, (level, row) in enumerate(wanted):
        x = border[i].astype(BF16)
        if row < 2:
            top_ref[row, level] = x
        else:
            bottom_ref[row - rows + 2, level] = x
        if row in (0, rows - 1):
            from_row = lane // 2 == 2 * level + (1 if row == 0 else 0)
            select = jnp.where((sub == column) & from_row, 1.0, 0.0).astype(BF16)
            spread_out += jnp.dot(x, select, preferred_element_type=F32)
    packed = jnp.where(own_lanes(padded, cells, width), spread_out, 0.0)
    corner_ref[...] = jnp.sum(packed.reshape(padded // 8, 8, cells), axis=1).astype(BF16)
    finish(fetch([top_ref, bottom_ref, corner_ref], [top_any, bottom_any, corner_any], sems))


def border_rows(planes, padded, levels, rows):
    cells = planes.shape[3]
    line = jax.ShapeDtypeStruct((2, levels, padded, cells), BF16)
    corner = jax.ShapeDtypeStruct((padded // 8, cells), BF16)
    return pl.pallas_call(
        functools.partial(row_kernel, rows),
        out_shape=(line, line, corner),
        in_specs=here(1),
        out_specs=tuple(here(3)),
        scratch_shapes=[
            pltpu.VMEM((4 * levels, padded, cells), F32), *buffers([line, line, corner]),
            pltpu.SemaphoreType.DMA((4 * levels,)),
        ],
        compiler_params=params(BIG),
        cost_estimate=pl.CostEstimate(flops=planes.size, bytes_accessed=planes.size, transcendentals=0),
        name="border_rows",
    )(planes)


def load_planes(source, target, sems):
    species = source.shape[0]
    copies = []
    for k in range(source.shape[1]):
        copy = pltpu.make_async_copy(source.at[:, k, 0, :], target.at[k, pl.ds(0, species), :], sems.at[k])
        copy.start()
        copies.append(copy)
    return copies


def column_kernel(levels, tracer_any, planes_any, right_ref, left_ref, planes, total, picker, sems, out_sems):
    count, padded, cells = planes.shape
    rows = count // levels
    load_planes(tracer_any, planes, sems)
    total[...] = jnp.zeros_like(total)
    picker[...] = jnp.zeros_like(picker)
    sub, lane = sublanes((16, 2 * cells)), lanes((16, 2 * cells))

    def one_level(level, carry):
        for row in range(rows):
            pltpu.make_async_copy(
                tracer_any.at[:, level * rows + row, 0, :],
                planes.at[level * rows + row, pl.ds(0, tracer_any.shape[0]), :],
                sems.at[level * rows + row],
            ).wait()
        part = pl.ds(level * rows, rows)
        pltpu.make_async_copy(planes.at[part], planes_any.at[part], out_sems.at[level]).start()
        for row in range(0, rows, 2):
            pair = []
            for h in range(2):
                k = level * rows + row + h
                pair.append(planes[k].astype(BF16))
                low = (sub < 2) & (lane == cells + 2 * k + sub)
                high = (sub >= 14) & (lane == 2 * k + sub - 14)
                picker[row // 2, pl.ds(h * cells, 16), :] = jnp.where(low, 1.0, 0.0).astype(BF16)
                picker[row // 2, pl.ds((h + 1) * cells - 16, 16), :] = jnp.where(high, 1.0, 0.0).astype(BF16)
            both = jnp.concatenate(pair, axis=1)
            total[...] += jnp.dot(both, picker[row // 2], preferred_element_type=F32)
        return carry

    lax.fori_loop(0, levels, one_level, 0)
    for level in range(levels):
        part = pl.ds(level * rows, rows)
        pltpu.make_async_copy(planes.at[part], planes_any.at[part], out_sems.at[level]).wait()
    right_ref[...] = total[:, 0:cells].astype(BF16)
    left_ref[...] = total[:, cells:].astype(BF16)


def columns(planes, padded, levels):
    _, count, _, cells = planes.shape
    side = jax.ShapeDtypeStruct((padded, cells), BF16)
    return pl.pallas_call(
        functools.partial(column_kernel, levels),
        out_shape=(
            jax.ShapeDtypeStruct((count, padded, cells), F32), side, side,
        ),
        in_specs=here(1),
        out_specs=(*here(1), *[pl.BlockSpec(memory_space=VMEM)] * 2),
        scratch_shapes=[
            pltpu.VMEM((count, padded, cells), F32),
            pltpu.VMEM((padded, 2 * cells), F32), pltpu.VMEM((count // levels // 2, 2 * cells, 2 * cells), BF16),
            pltpu.SemaphoreType.DMA((count,)), pltpu.SemaphoreType.DMA((levels,)),
        ],
        compiler_params=params(COL),
        cost_estimate=pl.CostEstimate(flops=12 * planes.size, bytes_accessed=4 * planes.size, transcendentals=0),
        name="columns",
    )(planes)


def softplus(x):
    return jnp.maximum(x, jnp.log(1.0 + jnp.exp(jnp.minimum(x, 60.0))))


def five_weights(face_x, face_x_low, face_y, face_y_low):
    up = -jnp.minimum(face_x, 0.0)
    down = jnp.maximum(face_x_low, 0.0)
    right = -jnp.minimum(face_y, 0.0)
    left = jnp.maximum(face_y_low, 0.0)
    stay = (
        1.0
        - (jnp.maximum(face_x, 0.0) - jnp.minimum(face_x_low, 0.0))
        - (jnp.maximum(face_y, 0.0) - jnp.minimum(face_y_low, 0.0))
    )
    return stay, up, down, left, right


def spread(x, level, count):
    return jnp.broadcast_to(x[level : level + 1], (count, x.shape[1]))


def make_weights(levels, line, west, east, inner, side, edge):
    rows = len(line) - 3
    fields, cells = line[0].shape
    lane = lanes((fields, cells))
    own_right = jnp.zeros((fields, cells), F32)
    for i in range(2, rows + 2):
        own_right = jnp.where(lane // 2 == i, turn(line[i], 2 * i - (cells - 2)), own_right)
    for i in range(1, rows + 3):
        now, low = line[i], line[i - 1]
        face_y_low = jnp.where(lane == 0, turn(west, -(2 * i + 1)), turn(now, 1))[levels:]
        five = five_weights(now[:levels], low[:levels], now[levels:], face_y_low)
        for level in range(levels):
            for c in range(3):
                inner[level, i - 1, c] = spread(five[c], level, 8)
            for c in range(2):
                side[level, i - 1, c] = spread(five[3 + c], level, 16).astype(BF16)
    odd = lane % 2 == 1
    middle = jnp.where(odd, west, east)
    lower = turn(middle, 2)
    y_low = jnp.where(odd, turn(west, 1), turn(own_right, -1))
    stay, up, down, left, right = five_weights(
        middle[:levels], lower[:levels], middle[levels:], y_low[levels:]
    )
    odd = odd[:levels]
    outer_w = jnp.where(odd, left, right)
    inner_w = jnp.where(odd, right, left)
    lane8 = lanes((8, cells))
    span = cells // levels
    for c, x in enumerate((stay, up, down, outer_w, inner_w)):
        out = jnp.zeros((8, cells), F32)
        for level in range(levels):
            out = jnp.where(lane8 // span == level, turn(spread(x, level, 8), level * span - 4), out)
        edge[c] = out


def place_corners(levels, came, corner_ref):
    padded, cells = corner_ref.shape
    width = 4 * levels
    span = cells // levels
    mine = own_lanes(padded, cells, width)
    parts, picks = [], []
    sub, lane = sublanes((cells, cells)) % width, lanes((cells, cells))
    for n, x in enumerate(came):
        x = jnp.broadcast_to(x.astype(F32)[:, None, :], (padded // 8, 8, cells))
        parts.append(jnp.where(mine, x.reshape(padded, cells), 0.0).astype(BF16))
        target = sub // 4 * span + (1, 0, span - 1, span - 2)[n]
        picks.append(jnp.where((sub % 4 == n) & (lane == target), 1.0, 0.0).astype(BF16))
    both = jnp.dot(
        jnp.concatenate(parts, axis=1), jnp.concatenate(picks, axis=0), preferred_element_type=F32
    )
    corner_ref[...] = both.astype(BF16)


def side_columns(rows, levels, right_ref, left_ref, west_ref, east_ref, edge, mid_ref, corner_ref, next_ref):
    padded, cells = right_ref.shape
    span = cells // levels
    lane = lanes((16, cells))
    odd = lane % 2 == 1
    row_of = (lane % span) // 2

    def group(g, carry):
        part = pl.ds(pl.multiple_of(g * 16, 16), 16)
        lo, hi = west_ref[part, :].astype(F32), east_ref[part, :].astype(F32)
        own_r, own_l = right_ref[part, :].astype(F32), left_ref[part, :].astype(F32)
        corner = corner_ref[part, :].astype(F32)
        weights = [jnp.concatenate([edge[c]] * 2, axis=0) for c in range(5)]
        mid = jnp.where(odd, lo, hi)
        outside = jnp.where(odd, turn(lo, 1), turn(hi, -1))
        inside = jnp.where(odd, turn(own_l, 1), turn(own_r, -1))
        above = jnp.where(row_of == rows - 1, corner, turn(mid, -2))
        below = jnp.where(row_of == 0, corner, turn(mid, 2))
        mid_ref[part, :] = mid.astype(BF16)
        after = (
            weights[0] * mid + weights[1] * above + weights[2] * below
            + weights[3] * outside + weights[4] * inside
        )
        next_ref[part, :] = after.astype(BF16)
        return carry

    lax.fori_loop(0, padded // 16, group, 0, unroll=8)


def read_labels(came_ref, label_v, beside):
    owners, _, cells = came_ref.shape
    tail = came_ref.shape[1] - 32

    def read(d, sums):
        x = came_ref[d, pl.ds(tail, 32), :].astype(F32)
        label_v[pl.ds(d, 1), :] = x[0:1].astype(jnp.int32)
        return sums + x

    beside[...] = lax.fori_loop(0, owners, read, jnp.zeros((32, cells), F32), unroll=16)


def add_slots(came_ref, label_s, total):
    owners = came_ref.shape[0]
    levfields = (came_ref.shape[1] - 32) // CAP
    rows = total.shape[0] // levfields - 1

    def add(d, carry):
        for k in range(CAP):
            at = pl.multiple_of(label_s[d, 2 * rows + 8 + k] * levfields, 8)
            total[pl.ds(at, levfields), :] += came_ref[d, pl.ds(k * levfields, levfields), :].astype(F32)
        return carry

    lax.fori_loop(0, owners, add, 0, unroll=16)


def light_of(levels, optical):
    depth = softplus(optical)
    parts, running = [], jnp.zeros((1, depth.shape[1]), F32)
    for level in range(levels):
        running = running + depth[level : level + 1]
        parts.append(jnp.exp(-running))
    return jnp.concatenate(parts, axis=0)


def advect_kernel(
    levels, planes_any, below_any, above_any, right_any, left_any, west_any, east_any,
    came_ref, rate_any, around_any, out_any, tile_any,
    planes, below_ref, above_ref, right_ref, left_ref, west_ref, east_ref,
    rate_ref,
    tile_ref, total, factor, label_v, label_s, ghost,
    inner, side, edge, mid_ref, corner_ref, next_ref, matrix, low_mask, high_mask, once, once16,
    plane_sems, in_sems, out_sems,
):
    levfields, rows, cells = tile_ref.shape
    padded = planes.shape[1]
    species = out_any.shape[0]
    span = cells // levels
    small = fetch(
        [rate_any, west_any, east_any, right_any, left_any, below_any, above_any],
        [rate_ref, west_ref, east_ref, right_ref, left_ref, below_ref, above_ref], in_sems,
    )
    parts = [pl.ds(level * rows, rows) for level in range(levels)]
    sub, lane = sublanes((cells, cells)), lanes((cells, cells))
    fetch([planes_any.at[p] for p in parts], [planes.at[p] for p in parts], plane_sems)
    read_labels(came_ref, label_v, ghost)
    label_copy = fetch([label_v], [label_s], in_sems.at[pl.ds(len(small), 1)])
    total[...] = jnp.zeros_like(total)
    low_mask[...] = jnp.where(sub == lane - 1, 1.0, 0.0).astype(BF16)
    high_mask[...] = jnp.where(sub == lane + 1, 1.0, 0.0).astype(BF16)
    finish(small)
    packed = padded // 8
    place_corners(levels, [
        ref[pl.ds(padded + n * packed, packed), :] for n in range(2) for ref in (west_ref, east_ref)
    ], corner_ref)
    finish(label_copy)
    add_slots(came_ref, label_s, total)
    for fl in range(levfields):
        for r in range(0, rows, 8):
            tile_ref[fl, pl.ds(r, 8), :] = total[pl.ds(r * levfields + fl, 8, stride=levfields), :]
    tile_copy = fetch([tile_ref], [tile_any], in_sems)
    fields = 2 * levels
    ghosts = 0.3 * jnp.tanh(ghost[...])
    line = [ghosts[24:32], ghosts[8:16]]
    for r in range(rows):
        line.append(0.3 * jnp.tanh(total[pl.ds(r * levfields, fields), :]))
        x = total[pl.ds(r * levfields, levfields), :]
        light = light_of(levels, x[fields : fields + levels])
        x = jnp.concatenate([x, light, jnp.zeros((16 - levels, cells), F32)], axis=0)
        high = x.astype(BF16)
        rest = (x - high.astype(F32)).astype(BF16)
        factor[r // 2, :, pl.ds(r % 2 * cells, cells)] = jnp.concatenate([high, rest, high], axis=0)
    line.append(ghosts[16:24])
    make_weights(levels, line, ghosts[0:8], turn(ghosts[0:8], cells // 2), inner, side, edge)
    side_columns(rows, levels, right_ref, left_ref, west_ref, east_ref, edge, mid_ref, corner_ref, next_ref)
    sub16, lane16 = sublanes((16, cells)), lanes((16, cells))

    def set_matrix(level, i):
        left, right = side[level, i + 1, 0], side[level, i + 1, 1]
        for t in range(cells // 16):
            at = pl.ds(16 * t, 16)
            matrix[i + 1, at, :] = low_mask[at, :] * left + high_mask[at, :] * right
        matrix[i + 1, pl.ds(cells, cells), :] = jnp.zeros((cells, cells), BF16)
        p = 2 * min(max(i, 0), rows - 1)
        tile = jnp.where(
            (sub16 == p % 16 + 1) & (lane16 == 0), left.astype(F32),
            jnp.where((sub16 == p % 16) & (lane16 == cells - 1), right.astype(F32), 0.0),
        )
        at = pl.multiple_of(cells + level * span + p // 16 * 16, 16)
        matrix[i + 1, pl.ds(at, 16), :] = tile.astype(BF16)

    def weighted(weights, x, up, down):
        count = x.shape[0] // 8
        stay, up_w, down_w = (w[None] for w in weights)
        x, up, down = (v.reshape(count, 8, cells) for v in (x, up, down))
        return (stay * x + up_w * up + down_w * down).reshape(count * 8, cells)

    def send(level, first, last):
        for r in range(first, last):
            k = level * rows + r
            pltpu.make_async_copy(
                planes.at[k, pl.ds(0, species), :], out_any.at[:, k, 0, :], out_sems.at[k]
            ).start()

    def one_level(level, carry):
        part = pl.ds(level * rows, rows)
        pltpu.make_async_copy(planes_any.at[part], planes.at[part], plane_sems.at[level]).wait()
        for i in range(-1, rows + 1):
            set_matrix(level, i)

        def half(b, carry):
            part = pl.ds(pl.multiple_of(b * HALF, HALF), HALF)

            def before(i):
                if i < 0:
                    return below_ref[i + 2, level, part, :].astype(F32)
                if i >= rows:
                    return above_ref[i - rows, level, part, :].astype(F32)
                return planes[level * rows + i, part, :]

            beside_next = next_ref[part, :]
            for i in range(-1, rows + 1):
                x = before(i)
                beside = (mid_ref if 0 <= i < rows else corner_ref)[part, :]
                both = jnp.concatenate([x.astype(BF16), beside], axis=1)
                across = jnp.dot(both, matrix[i + 1], preferred_element_type=F32)
                weights = [inner[level, i + 1, c] for c in range(3)]
                x = weighted(weights, x, before(i + 1), before(i - 1)) + across
                once[i + 1] = x
                if 0 <= i < rows:
                    once16[i] = x.astype(BF16)
            for i in range(rows):
                both = jnp.concatenate([once16[i], beside_next], axis=1)
                across = jnp.dot(both, matrix[i + 1], preferred_element_type=F32)
                weights = [inner[level, i + 1, c] for c in range(3)]
                moved = weighted(weights, once[i + 1], once[i + 2], once[i]) + across
                if i % 2 == 0:
                    exponents = jnp.dot(rate_ref[level, part, :], factor[i // 2], preferred_element_type=F32)
                exponent = exponents[:, i % 2 * cells : (i % 2 + 1) * cells]
                planes[level * rows + i, part, :] = moved * pl.reciprocal(
                    1.0 + softplus(exponent), approx=False
                )
                if i == rows // 2 and HALF == padded:
                    send(level, 0, rows // 2)
            return carry

        lax.fori_loop(0, padded // HALF, half, 0)
        send(level, rows // 2 if HALF == padded else 0, rows)
        return carry

    lax.fori_loop(0, levels, one_level, 0)
    finish(tile_copy)
    for k in range(levels * rows):
        pltpu.make_async_copy(
            planes.at[k, pl.ds(0, species), :], out_any.at[:, k, 0, :], out_sems.at[k]
        ).wait()


def advect(planes, below, above, right, left, west, east, came, rate, around, species):
    levels, padded, cells = below.shape[1:]
    count = planes.shape[0]
    rows = count // levels
    owners = came.shape[0]
    levfields = (came.shape[1] - 32) // CAP
    tile = jax.ShapeDtypeStruct((levfields, rows, cells), F32)
    small = [below, above, right, left, west, east, rate]
    column = pltpu.VMEM((padded, cells), BF16)
    square = pltpu.VMEM((cells, cells), BF16)
    return pl.pallas_call(
        functools.partial(advect_kernel, levels),
        out_shape=(jax.ShapeDtypeStruct((species, count, 1, cells), F32), tile),
        in_specs=here(len(small)) + [pl.BlockSpec(memory_space=VMEM)] + here(2),
        out_specs=tuple(here(2)),
        scratch_shapes=[
            pltpu.VMEM((count, padded, cells), F32),
            *buffers(small), *buffers([tile]),
            pltpu.VMEM(((rows + 1) * levfields, cells), F32),
            pltpu.VMEM((rows // 2, rate.shape[2], 2 * cells), BF16),
            pltpu.VMEM((owners, cells), jnp.int32), pltpu.SMEM((owners, cells), jnp.int32),
            pltpu.VMEM((32, cells), F32),
            pltpu.VMEM((levels, rows + 2, 3, 8, cells), F32),
            pltpu.VMEM((levels, rows + 2, 2, 16, cells), BF16),
            pltpu.VMEM((5, 8, cells), F32),
            column, column, column,
            pltpu.VMEM((rows + 2, 2 * cells, cells), BF16),
            square, square,
            pltpu.VMEM((rows + 2, HALF, cells), F32),
            pltpu.VMEM((rows, HALF, cells), BF16),
            pltpu.SemaphoreType.DMA((levels,)), pltpu.SemaphoreType.DMA((len(small) + 1,)),
            pltpu.SemaphoreType.DMA((count,)),
        ],
        compiler_params=params(ADV),
        cost_estimate=pl.CostEstimate(
            flops=60 * planes.size, bytes_accessed=8 * planes.size, transcendentals=3 * planes.size
        ),
        name="advect",
    )(planes, *small[:-1], came, rate, around)


def arrived_kernel(*refs):
    refs[-1][...] = jnp.zeros_like(refs[-1])


def arrived(arrays):
    return pl.pallas_call(
        arrived_kernel,
        out_shape=jax.ShapeDtypeStruct((8, 128), F32),
        in_specs=here(len(arrays)),
        compiler_params=params(1),
        cost_estimate=pl.CostEstimate(flops=MIB, bytes_accessed=0, transcendentals=0),
        name="arrived",
    )(*arrays)


def rate_factors(rate_coef, photo_coef, levels, padded):
    species, fields = rate_coef.shape
    same = jnp.eye(levels, dtype=F32)
    by_field = rate_coef[None, :, :, None] * same[:, None, None, :]
    by_light = photo_coef[None, :, None] * same[:, None, :]
    table = jnp.concatenate([by_field.reshape(levels, species, fields * levels), by_light], axis=2)
    table = jnp.pad(table, ((0, 0), (0, padded - species), (0, 64 - table.shape[2])))
    high = lax.reduce_precision(table, 8, 7)
    rest = (table - high).astype(BF16)
    high = high.astype(BF16)
    return jnp.concatenate([high, high, rest], axis=2)


def shift(x, axis, by):
    count = lax.axis_size(axis)
    return lax.ppermute(x, axis, [(i, (i + by) % count) for i in range(count)])


def local(met_src, intersection_weights, block_dest, block_row, tracers, rate_coef, photo_coef):
    n_face, n_tile = lax.axis_size("face"), lax.axis_size("tile")
    species, levels, rows, cells = tracers.shape
    padded = -(-species // HALF) * HALF
    tracer_planes = tracers.reshape(species, levels * rows, 1, cells)

    payload = regrid(block_dest, block_row, met_src, intersection_weights, n_face, n_tile, rows)
    payload, tracer_planes = lax.optimization_barrier((payload, tracer_planes))
    came = lax.all_to_all(payload, ("face", "tile"), split_axis=0, concat_axis=0, tiled=True)

    top, bottom, corner = border_rows(tracer_planes, padded, levels, rows)
    corner_below = shift(corner, "face", 1)
    corner_above = shift(corner, "face", -1)
    below = shift(bottom, "face", 1)
    above = shift(top, "face", -1)
    tracer_planes, top, bottom = lax.optimization_barrier((tracer_planes, top, bottom))
    planes, right, left = columns(tracer_planes, padded, levels)
    west = shift(jnp.concatenate([right, corner_below, corner_above], axis=0), "tile", 1)
    east = shift(jnp.concatenate([left, corner_below, corner_above], axis=0), "tile", -1)
    beside = arrived([west, east])
    around = arrived([below, above, beside])
    rate = rate_factors(rate_coef, photo_coef, levels, padded)
    out, met_tile = advect(planes, below, above, right, left, west, east, came, rate, around, species)
    fields = rate_coef.shape[1]
    return met_tile.reshape(fields, levels, rows, cells), out.reshape(species, levels, rows, cells)


def solution(mesh):
    return jax.shard_map(
        local,
        mesh=mesh,
        in_specs=(
            P(("face", "tile"), None, None),
            P(("face", "tile"), None, None),
            P(("face", "tile")),
            P(("face", "tile")),
            P(None, None, "face", "tile"),
            P(),
            P(),
        ),
        out_specs=(P(None, None, "face", "tile"), P(None, None, "face", "tile")),
        check_vma=False,
    )
```
